512 devices in a mesh: tm: 16 (over z), op: 8 (over x, core), spin: 4 (over y).
Axes of the slice: x: 4, y: 4, z: 16, core: 2. Of those that a mesh axis runs over, the one named last changes fastest.
Arguments:
- pairs: int32 [16, 2], replicated, may hold values from 0 to 15, as said below
- elements: bfloat16 [16, 16, 64, 4096], P('tm', 'op', 'spin'), may hold values from -0.119628906 to 0.119628906
- perambs: bfloat16 [16, 16, 3, 4096], P(None, 'spin'), may hold values from -0.75 to 0.75
Outputs:
- correlator: float32 [16, 16, 16], P('tm')
The draws below stay inside these ranges and needn't reach their ends.
Inputs may be any that keep to these rules, and one draw needn't show every extreme that they name: Column 0 is a pair's source time and column 1 its sink time, never equal. No time slice is the sink of more than 2 pairs, and some time slice is the sink of exactly 2.
All inputs are finite; a program needn't handle non-finite values.
Results may differ from the reference program's by a relative error of at most 0.007.
Values may be sent and summed in bfloat16 or wider, within the bound.
A program may use at most 64 MiB of HBM per device.

```python
import jax
import jax.numpy as jnp
from jax import lax

MODES = 64
OPS = 16
T_DEV = 1
SB_DEV = 4
MOST = 2
TIMES = 16
PAIRS = 16
GROUPS = 4
SPINB = 16
N_TM = 16


def draw_pairs(key, part):
    key = jax.random.fold_in(key, 7)
    key_join, key_perm, key_slice, key_back, key_order = jax.random.split(key, 5)
    coins = jax.random.randint(key_join, (PAIRS,), 0, 2)
    places = jnp.arange(PAIRS, dtype=jnp.int32)
    coins = jnp.where(places == 1, 1, coins)

    def advance(state, item):
        holder, filled = state
        joined = (item > 0) & (filled < MOST)
        holder = jnp.where(joined, holder, holder + 1)
        filled = jnp.where(joined, filled + 1, 1)
        return ((holder, filled), holder)
    start_state = (jnp.array(-1, jnp.int32), jnp.array(MOST, jnp.int32))
    final_state, holders = lax.scan(advance, start_state, coins.astype(jnp.int32))
    devices_perm = jax.random.permutation(key_perm, N_TM).astype(jnp.int32)
    sink_device = devices_perm[holders]
    sink_time = (sink_device * T_DEV + jax.random.randint(key_slice, (PAIRS,), 0, T_DEV)).astype(jnp.int32)
    source_time = ((sink_time - 1 - jax.random.randint(key_back, (PAIRS,), 0, TIMES - 1)) % TIMES).astype(jnp.int32)
    top_source = jnp.where(sink_time[0] == TIMES - 1, 0, TIMES - 1).astype(jnp.int32)
    low_source = jnp.where(sink_time[1] == 0, TIMES - 1, 0).astype(jnp.int32)
    source_time = jnp.where(places == 0, top_source, source_time)
    source_time = jnp.where(places == 1, low_source, source_time)
    listed = jnp.stack([source_time, sink_time], axis=1).astype(jnp.int32)
    shuffle = jax.random.permutation(key_order, PAIRS)
    return listed[shuffle]


def levels(own_key, shape, cuts, low, largest):
    def one(axis_at, blocks):
        heights = jax.random.uniform(jax.random.fold_in(jax.random.fold_in(own_key, 6), axis_at), (blocks,), jnp.float32, low / len(cuts), largest / len(cuts))
        return jnp.repeat(jnp.exp(heights), shape[axis_at] // blocks).reshape((-1,) + (1,) * (len(shape) - axis_at - 1))

    level = one(*cuts[0])
    for cut in cuts[1:]:
        level = level * one(*cut)
    return level


def centred(own_key, dims, spread, limit, cuts=(), kind=jnp.bfloat16):
    loudness = levels(own_key, dims, cuts, -0.22, 0.18) if cuts else 1.0
    values = jax.random.normal(own_key, dims, jnp.float32) * spread * loudness
    return jnp.minimum(jnp.maximum(values, -limit), limit).astype(kind)


def setup_inputs(seed: int = 0) -> dict:
    keys = jax.random.split(jax.random.key(seed), 4)
    return {
        "pairs": draw_pairs(jax.random.fold_in(keys[3], 71), 0),
        "elements": centred(keys[1], (TIMES, OPS, MODES, MODES * MODES), 0.02, 0.119628906, ((0, 16), (1, 8), (2, 4))),
        "perambs": centred(keys[2], (PAIRS, SPINB, 3, MODES * MODES), MODES ** -0.5, 0.75, ((1, 4),)),
    }


def apply_modes(source, blocks):
    mats = blocks.astype(jnp.float32).reshape(SB_DEV, 3, MODES, MODES)
    first_mode = jnp.einsum('bxa,jan->bjxn', mats[:, 0], source.astype(jnp.float32)).astype(jnp.bfloat16)
    first_five = first_mode.astype(jnp.float32).reshape(SB_DEV, OPS, MODES, MODES, MODES)
    second_mode = jnp.einsum('byq,bjxqz->bjxyz', mats[:, 1], first_five).astype(jnp.bfloat16)
    third_mode = jnp.einsum('bzc,bjxyc->jxyz', mats[:, 2], second_mode.astype(jnp.float32))
    return third_mode.astype(jnp.bfloat16).reshape(OPS, MODES, MODES * MODES)


def reference(pairs, elements, perambs):
    def one_pair(index):
        source = lax.dynamic_index_in_dim(elements, pairs[index, 0], 0, keepdims=False)
        sink = lax.dynamic_index_in_dim(elements, pairs[index, 1], 0, keepdims=False)
        spin_blocks = lax.dynamic_index_in_dim(perambs, index, 0, keepdims=False)
        result = jnp.zeros((OPS, OPS), jnp.float32)
        for group in range(GROUPS):
            blocks = spin_blocks[group * SB_DEV:(group + 1) * SB_DEV]
            product = apply_modes(source, blocks)
            result = result + jnp.einsum('ixn,jxn->ij', sink.astype(jnp.float32), product.astype(jnp.float32))
        return result

    return lax.map(one_pair, jnp.arange(PAIRS, dtype=jnp.int32))
```

```python
import functools

import jax
import jax.numpy as jnp
from jax import lax
from jax.experimental import pallas as pl
from jax.experimental.pallas import tpu as pltpu
from jax.sharding import PartitionSpec as P

MESH = pl.DeviceIdType.MESH
F32 = jnp.float32
BF16 = jnp.bfloat16
NN = (((1,), (0,)), ((), ()))
NT = (((1,), (1,)), ((), ()))


def dot(a, b, dims=NN, precision=None):
    return lax.dot_general(a, b, dims, precision=precision, preferred_element_type=F32)


def iota(shape, axis):
    return lax.broadcasted_iota(jnp.int32, shape, axis)


def kernel(
    zn, pairs, elements, perambs, out,
    win, pv, s8, n64, qn, q0s, bd, q1r, v, t2, s3, prod, sink, rprod, rsink, part, core_part,
    pv_sem, own_recv, own_send, zr, zs, cr, cs, qr, qs, ar, asend, br, bsend, rr, rs, kr, ks,
):
    z, op, y = lax.axis_index("tm"), lax.axis_index("op"), lax.axis_index("spin")
    x, c = op // 2, lax.rem(op, 2)
    chip = x * 4 + y
    other = op + 1 - 2 * c
    up, down = lax.rem(z + 1, zn), lax.rem(z + zn - 1, zn)

    def remote(src, dst, send, recv, device):
        return pltpu.make_async_remote_copy(
            src_ref=src, dst_ref=dst, send_sem=send, recv_sem=recv, device_id=device, device_id_type=MESH
        )

    take_perambs = pltpu.make_async_copy(perambs, pv, pv_sem)
    take_perambs.start()

    barrier = pltpu.get_barrier_semaphore()

    def greet(i, carry):
        o, s = i // 4, lax.rem(i, 4)

        @pl.when(i != op * 4 + y)
        def _():
            pl.semaphore_signal(barrier, inc=1, device_id=(z, o, s), device_id_type=MESH)

        return carry

    lax.fori_loop(0, 32, greet, 0)
    for place in (up, down):
        pl.semaphore_signal(barrier, inc=1, device_id=(place, op, y), device_id_type=MESH)
    pl.semaphore_wait(barrier, 33)

    for k in range(2):
        target = 2 * c + k

        @pl.when(target == y)
        def _(k=k):
            pltpu.make_async_copy(elements.at[0, k], win.at[0, y], own_recv.at[lax.rem(y, 2)]).start()

        @pl.when(target != y)
        def _(k=k, target=target):
            remote(
                elements.at[0, k], win.at[0, y], own_send.at[k], own_recv.at[lax.rem(y, 2)],
                (z, 2 * x + y // 2, target),
            ).start()

    plus_hops, minus_hops = (zn // 2, zn // 2 - 1), (zn // 2 - 1, zn // 2)

    def to_core(slot, k):
        block = win.at[slot, 2 * c + k]
        return remote(block, block, cs.at[slot, k], cr.at[slot, k], (z, other, y))

    def from_core(slot, k):
        block = win.at[slot, 2 * (1 - c) + k]
        return remote(block, block, cs.at[slot, k], cr.at[slot, k], (z, other, y))

    def along(slot, hop, k, way):
        to_slot = hop if way == 0 else zn - hop
        return remote(
            win.at[slot, 2 * c + k], win.at[to_slot, 2 * c + k], zs.at[way, hop, k], zr.at[way, hop, k],
            ((up, down)[way], op, y),
        )

    def hand_on(hop, k):
        for way in range(2):
            hops = (plus_hops, minus_hops)[way]
            slot = 0 if hop == 0 else (hop if way == 0 else zn - hop)
            if hop <= hops[k]:
                if hop > 0:
                    along(slot, hop, k, way).wait_recv()
                if hop < hops[k]:
                    along(slot, hop + 1, k, way).start()
                if hop > 0 or way == 0:
                    to_core(slot, k).start()

    for k in range(2):
        pltpu.make_async_copy(elements.at[0, k], win.at[0, 2 * c + k], own_recv.at[k]).wait()
        hand_on(0, k)

    pair = z
    lane = iota((32, 128), 1) < 64
    take_perambs.wait()

    def flat(b, carry):
        rows = pv[pair, b].astype(F32)
        for t in range(32):
            s8[t * 8:t * 8 + 3, :] = rows[:, t * 128:(t + 1) * 128]
        for l in range(3):
            q = s8[pl.ds(l, 32, stride=8), :]
            r = pltpu.roll(q, 64, 1)
            n64[pl.ds(0, 32, stride=2), :] = jnp.where(lane, q, r)
            n64[pl.ds(1, 32, stride=2), :] = jnp.where(lane, r, q)
            qn[y, b, l] = n64[...].astype(BF16)
        return carry

    lax.fori_loop(0, 4, flat, 0)
    for d in range(1, 4):
        remote(qn.at[y], qn.at[y], qs.at[d], qr.at[d], (z, op, lax.rem(y + d, 4))).start()
    for k in range(2):
        hand_on(1, k)
    for d in range(1, 4):
        remote(qn.at[y], qn.at[lax.rem(y + 4 - d, 4)], qs.at[d], qr.at[d], (z, op, y)).wait_recv()
    for k in range(2):
        hand_on(2, k)

    bd[...] = jnp.zeros_like(bd)
    low = iota((64, 128), 1) < 64

    def blocks(b, carry):
        bq, bb = b // 4, lax.rem(b, 4)
        q0s[pl.ds(b * 32, 32), :] = qn[bq, bb, 0, pl.ds(32 * c, 32), :]
        q2 = qn[bq, bb, 2]
        none = jnp.zeros_like(q2)
        for k in range(4):
            half = jnp.where(low, q2, none) if k % 2 == 0 else jnp.where(low, none, q2)
            bd[b, k * 64:(k + 1) * 64, (k // 2) * 128:(k // 2 + 1) * 128] = half
        return carry

    lax.fori_loop(0, 16, blocks, 0)
    for k in range(2):
        hand_on(3, k)

    rowq, lanel = iota((128, 128), 0), iota((128, 128), 1)
    for g in range(4):
        for lo in range(2):
            acc = jnp.zeros((64, 128), F32)
            for bb in range(4):
                spot = (rowq < 64) & (lax.rem(rowq, 2) == lo) & (lanel == bb * 32 + rowq // 2)
                acc += dot(qn[g, bb, 1], jnp.where(spot, 1.0, 0.0).astype(BF16))
            q1r[lo * 64:(lo + 1) * 64, g * 128:(g + 1) * 128] = acc.astype(BF16)

    for hop in range(4, zn // 2 + 1):
        for k in range(2):
            hand_on(hop, k)
    for slot in range(zn):
        for k in range(2):
            from_core(slot, k).wait_recv()

    source_at = lax.rem(z + zn - pairs[pair, 0], zn)
    sink_at = lax.rem(z + zn - pairs[pair, 1], zn)

    def cut(i, carry):
        k, part_at = i // 8, lax.rem(i, 8)
        sink[i] = win[sink_at, 2 * c + k, :, pl.ds(pl.multiple_of(part_at * 512, 512), 512)]
        return carry

    lax.fori_loop(0, 16, cut, 0)

    def place(xx, yy):
        return lax.rem(yy, 2) * 8 + 2 * xx + yy // 2

    def spread(data, landed, send, recv):
        def one(d, carry):
            xx, yy = lax.rem(x + d // 4, 4), lax.rem(y + lax.rem(d, 4), 4)
            remote(
                data.at[place(xx, yy)], landed.at[chip], send.at[d], recv.at[chip], (z, 2 * xx + c, yy)
            ).start()
            return carry

        lax.fori_loop(1, 16, one, 0)
        landed[chip] = data[place(x, y)]

    def collect(landed, send, recv):
        def one(d, carry):
            e = lax.rem(chip + d, 16)
            remote(landed.at[e], landed.at[e], send.at[d], recv.at[e], (z, op, y)).wait_recv()
            return carry

        lax.fori_loop(1, 16, one, 0)

    spread(sink, rsink, bsend, br)

    def step_one(n, carry):
        columns = win[source_at, :, :, pl.ds(pl.multiple_of(n * 256, 256), 256)].reshape(64, 256)
        first = dot(q0s[:, :64], columns).astype(BF16)
        v[:, n] = first.reshape(16, 32, 256)
        return carry

    lax.fori_loop(0, 16, step_one, 0)

    def step_two(b, carry):
        second = dot(v[b].reshape(512, 256), bd[b], NT)
        for n in range(16):
            for h in range(2):
                start = pl.multiple_of((b * 32 + n * 2 + h) * 32, 32)
                t2[pl.ds(start, 32), :] = second[n * 32:(n + 1) * 32, h * 128:(h + 1) * 128]
        return carry

    lax.fori_loop(0, 16, step_two, 0)

    def step_three(u, carry):
        left = t2[pl.ds(u, 512, stride=32), :].astype(BF16)
        right = t2[pl.ds(u + 16, 512, stride=32), :].astype(BF16)
        both = dot(q1r[...], jnp.concatenate([left, right], axis=1))
        even = both[:64, :128] + pltpu.roll(both[64:, :128], 64, 1)
        odd = pltpu.roll(both[:64, 128:], 64, 1) + both[64:, 128:]
        s3[pl.ds(pl.multiple_of(u * 64, 64), 64), :] = jnp.where(low, even, odd)
        return carry

    lax.fori_loop(0, 16, step_three, 0)
    lane16 = iota((16, 128), 1) < 64

    def natural(p, carry):
        for w in range(4):
            t = p * 4 + w
            a = s3[pl.ds(2 * t, 16, stride=64), :]
            b = s3[pl.ds(2 * t + 1, 16, stride=64), :]
            prod[p, :, w * 128:(w + 1) * 128] = jnp.where(lane16, a, pltpu.roll(b, 64, 1)).astype(BF16)
            prod[8 + p, :, w * 128:(w + 1) * 128] = jnp.where(lane16, pltpu.roll(a, 64, 1), b).astype(BF16)
        return carry

    lax.fori_loop(0, 8, natural, 0)
    spread(prod, rprod, asend, ar)
    collect(rsink, bsend, br)
    collect(rprod, asend, ar)

    grid = dot(rsink[...].reshape(256, 512), rprod[...].reshape(256, 512), NT)
    r256, l256 = iota((256, 256), 0), iota((256, 256), 1)
    same = jnp.where(lax.rem(r256, 16) == lax.rem(l256, 16), grid, 0.0)
    by_row = jnp.sum(same.reshape(16, 16, 256), axis=1)
    gl, gj = iota((256, 128), 0), iota((256, 128), 1)
    gather = jnp.where(gl // 16 == lax.rem(gj, 16), 1.0, 0.0).astype(F32)
    table = dot(by_row, gather, precision=lax.Precision.HIGHEST)
    ti, tl = iota((16, 128), 0), iota((16, 128), 1)
    mine = jnp.where(tl // 16 == lax.rem(ti, 8), table, 0.0)
    part[chip] = jnp.sum(mine.reshape(2, 8, 128), axis=1)

    def tell(d, carry):
        xx, yy = lax.rem(x + d // 4, 4), lax.rem(y + lax.rem(d, 4), 4)
        remote(part.at[chip], part.at[chip], rs.at[d], rr.at[chip], (z, 2 * xx + c, yy)).start()
        return carry

    lax.fori_loop(1, 16, tell, 0)
    collect(part, rs, rr)
    core_part[c] = jnp.sum(part[...], axis=0)
    swap = remote(core_part.at[c], core_part.at[c], ks, kr, (z, other, y))
    swap.start()
    swap.wait_send()
    remote(core_part.at[1 - c], core_part.at[1 - c], ks, kr, (z, other, y)).wait_recv()
    out[...] = core_part[0] + core_part[1]

    for k in range(2):
        @pl.when(2 * c + k != y)
        def _(k=k):
            remote(elements.at[0, k], win.at[0, y], own_send.at[k], own_recv.at[k], (z, op, y)).wait_send()

        for way in range(2):
            for hop in range(1, (plus_hops, minus_hops)[way][k] + 1):
                along(0, hop, k, way).wait_send()
        for slot in range(zn):
            to_core(slot, k).wait_send()
    for d in range(1, 4):
        remote(qn.at[y], qn.at[y], qs.at[d], qr.at[d], (z, op, y)).wait_send()

    def left(d, carry):
        remote(sink.at[0], rsink.at[0], bsend.at[d], br.at[0], (z, op, y)).wait_send()
        remote(prod.at[0], rprod.at[0], asend.at[d], ar.at[0], (z, op, y)).wait_send()
        remote(part.at[0], part.at[0], rs.at[d], rr.at[0], (z, op, y)).wait_send()
        return carry

    lax.fori_loop(1, 16, left, 0)


def solution(mesh):
    zn = mesh.shape["tm"]

    def body(pairs, elements, perambs):
        dma = pltpu.SemaphoreType.DMA
        result = pl.pallas_call(
            functools.partial(kernel, zn),
            out_shape=jax.ShapeDtypeStruct((2, 128), F32),
            in_specs=[
                pl.BlockSpec(memory_space=pltpu.SMEM),
                pl.BlockSpec(memory_space=pl.ANY),
                pl.BlockSpec(memory_space=pl.ANY),
            ],
            out_specs=pl.BlockSpec(memory_space=pltpu.VMEM),
            scratch_shapes=[
                pltpu.VMEM((zn, 4, 16, 4096), BF16),
                pltpu.VMEM((16, 4, 3, 4096), BF16),
                pltpu.VMEM((256, 128), F32),
                pltpu.VMEM((64, 128), F32),
                pltpu.VMEM((4, 4, 3, 64, 128), BF16),
                pltpu.VMEM((512, 128), BF16),
                pltpu.VMEM((16, 256, 256), BF16),
                pltpu.VMEM((128, 512), BF16),
                pltpu.VMEM((16, 16, 32, 256), BF16),
                pltpu.VMEM((16384, 128), F32),
                pltpu.VMEM((1024, 128), F32),
                pltpu.VMEM((16, 16, 512), BF16),
                pltpu.VMEM((16, 16, 512), BF16),
                pltpu.VMEM((16, 16, 512), BF16),
                pltpu.VMEM((16, 16, 512), BF16),
                pltpu.VMEM((16, 2, 128), F32),
                pltpu.VMEM((2, 2, 128), F32),
                dma, dma((2,)), dma((2,)),
                dma((2, zn, 2)), dma((2, zn, 2)), dma((zn, 2)), dma((zn, 2)),
                dma((4,)), dma((4,)),
                dma((16,)), dma((16,)), dma((16,)), dma((16,)), dma((16,)), dma((16,)),
                dma, dma,
            ],
            compiler_params=pltpu.CompilerParams(
                collective_id=0, has_side_effects=True, vmem_limit_bytes=56 * 1024 * 1024
            ),
        )(pairs, elements, perambs)
        return result.reshape(1, 16, 16)

    placed = (P(), P("tm", "op", "spin", None), P(None, "spin", None, None))
    return jax.shard_map(
        body, mesh=mesh, in_specs=placed, out_specs=P("tm", None, None), check_vma=False
    )
```

```python
import functools

import jax
import jax.numpy as jnp
from jax import lax
from jax.experimental import pallas as pl
from jax.experimental.pallas import tpu as pltpu
from jax.sharding import PartitionSpec as P

MESH = pl.DeviceIdType.MESH
F32 = jnp.float32
BF16 = jnp.bfloat16
NN = (((1,), (0,)), ((), ()))
NT = (((1,), (1,)), ((), ()))
PITCH = 40


def dot(a, b, dims=NN, precision=None):
    return lax.dot_general(a, b, dims, precision=precision, preferred_element_type=F32)


def iota(shape, axis):
    return lax.broadcasted_iota(jnp.int32, shape, axis)


def kernel(
    zn, pairs, elements, perambs, out,
    win, pv, s8, n64, qn, q0s, bd, q1r, v, t2, prod, sink, rprod, rsink, ks, kp, part, core_part,
    pv_sem, own_recv, own_send, zr, zs, cr, cs, qr, qs, ar, asend, br, bsend, rr, rs, xr, xs,
):
    z, op, y = lax.axis_index("tm"), lax.axis_index("op"), lax.axis_index("spin")
    x, c = op // 2, lax.rem(op, 2)
    chip = x * 4 + y
    other = op + 1 - 2 * c
    up, down = lax.rem(z + 1, zn), lax.rem(z + zn - 1, zn)

    def remote(src, dst, send, recv, device):
        return pltpu.make_async_remote_copy(
            src_ref=src, dst_ref=dst, send_sem=send, recv_sem=recv, device_id=device, device_id_type=MESH
        )

    take_perambs = pltpu.make_async_copy(perambs, pv, pv_sem)
    take_perambs.start()

    barrier = pltpu.get_barrier_semaphore()

    def greet(i, carry):
        o, s = i // 4, lax.rem(i, 4)

        @pl.when(i != op * 4 + y)
        def _():
            pl.semaphore_signal(barrier, inc=1, device_id=(z, o, s), device_id_type=MESH)

        return carry

    lax.fori_loop(0, 32, greet, 0)
    for place in (up, down):
        pl.semaphore_signal(barrier, inc=1, device_id=(place, op, y), device_id_type=MESH)
    pl.semaphore_wait(barrier, 33)

    for k in range(2):
        target = 2 * c + k

        @pl.when(target == y)
        def _(k=k):
            pltpu.make_async_copy(elements.at[0, k], win.at[0, y], own_recv.at[lax.rem(y, 2)]).start()

        @pl.when(target != y)
        def _(k=k, target=target):
            remote(
                elements.at[0, k], win.at[0, y], own_send.at[k], own_recv.at[lax.rem(y, 2)],
                (z, 2 * x + y // 2, target),
            ).start()

    plus_hops, minus_hops = (zn // 2, zn // 2 - 1), (zn // 2 - 1, zn // 2)

    def to_core(slot, k):
        block = win.at[slot, 2 * c + k]
        return remote(block, block, cs.at[slot, k], cr.at[slot, k], (z, other, y))

    def from_core(slot, k):
        block = win.at[slot, 2 * (1 - c) + k]
        return remote(block, block, cs.at[slot, k], cr.at[slot, k], (z, other, y))

    def along(slot, hop, k, way):
        to_slot = hop if way == 0 else zn - hop
        return remote(
            win.at[slot, 2 * c + k], win.at[to_slot, 2 * c + k], zs.at[way, hop, k], zr.at[way, hop, k],
            ((up, down)[way], op, y),
        )

    def hand_on(hop, k):
        for way in range(2):
            hops = (plus_hops, minus_hops)[way]
            slot = 0 if hop == 0 else (hop if way == 0 else zn - hop)
            if hop <= hops[k]:
                if hop > 0:
                    along(slot, hop, k, way).wait_recv()
                if hop < hops[k]:
                    along(slot, hop + 1, k, way).start()
                if hop > 0 or way == 0:
                    to_core(slot, k).start()

    for k in range(2):
        pltpu.make_async_copy(elements.at[0, k], win.at[0, 2 * c + k], own_recv.at[k]).wait()
        hand_on(0, k)

    pair = z
    lane = iota((32, 128), 1) < 64
    take_perambs.wait()

    def flat(l, carry):
        rows = pv[pair, l].astype(F32)
        for t in range(32):
            s8[t * 8:t * 8 + 4, :] = rows[:, t * 128:(t + 1) * 128]
        for b in range(4):
            q = s8[pl.ds(b, 32, stride=8), :]
            r = pltpu.roll(q, 64, 1)
            n64[pl.ds(0, 32, stride=2), :] = jnp.where(lane, q, r)
            n64[pl.ds(1, 32, stride=2), :] = jnp.where(lane, r, q)
            qn[y, b, l] = n64[...].astype(BF16)
        return carry

    lax.fori_loop(0, 3, flat, 0)
    for d in range(1, 4):
        remote(qn.at[y], qn.at[y], qs.at[d], qr.at[d], (z, op, lax.rem(y + d, 4))).start()
    for k in range(2):
        hand_on(1, k)
    for d in range(1, 4):
        remote(qn.at[y], qn.at[lax.rem(y + 4 - d, 4)], qs.at[d], qr.at[d], (z, op, y)).wait_recv()
    for k in range(2):
        hand_on(2, k)

    bd[...] = jnp.zeros_like(bd)
    low = iota((64, 128), 1) < 64

    def blocks(b, carry):
        bq, bb = b // 4, lax.rem(b, 4)
        q0s[pl.ds(b * 32, 32), :] = qn[bq, bb, 0, pl.ds(32 * c, 32), :]
        q2 = qn[bq, bb, 2]
        none = jnp.zeros_like(q2)
        for k in range(4):
            half = jnp.where(low, q2, none) if k % 2 == 0 else jnp.where(low, none, q2)
            bd[b, k * 64:(k + 1) * 64, (k // 2) * 128:(k // 2 + 1) * 128] = half
        return carry

    lax.fori_loop(0, 16, blocks, 0)
    for k in range(2):
        hand_on(3, k)

    rowq, lanel = iota((128, 128), 0), iota((128, 128), 1)
    for g in range(4):
        for lo in range(2):
            acc = jnp.zeros((64, 128), F32)
            for bb in range(4):
                spot = (rowq < 64) & (lax.rem(rowq, 2) == lo) & (lanel == bb * 32 + rowq // 2)
                acc += dot(qn[g, bb, 1], jnp.where(spot, 1.0, 0.0).astype(BF16))
            q1r[lo * 64:(lo + 1) * 64, g * 128:(g + 1) * 128] = acc.astype(BF16)

    for hop in range(4, zn // 2 + 1):
        for k in range(2):
            hand_on(hop, k)
    for slot in range(zn):
        for k in range(2):
            from_core(slot, k).wait_recv()

    source_at = lax.rem(z + zn - pairs[0, pair], zn)
    sink_at = lax.rem(z + zn - pairs[1, pair], zn)

    for k in range(2):
        def lift(t, carry, k=k):
            tile = win[sink_at, 2 * c + k, :, pl.ds(pl.multiple_of(t * 128, 128), 128)]
            t2[pl.ds(pl.multiple_of((k * 32 + t) * 24, 8), 16), :] = tile.astype(F32)
            return carry

        lax.fori_loop(0, 32, lift, 0, unroll=8)

    def chip_at(d):
        xx, yy = lax.rem(x + d // 4, 4), lax.rem(y + lax.rem(d, 4), 4)
        return xx * 4 + yy, (z, 2 * xx + c, yy)

    def cut(u, carry):
        sink[u] = t2[pl.ds(u, 64, stride=24), :].astype(BF16)
        return carry

    lax.fori_loop(0, 16, cut, 0, unroll=8)

    def post(data, landed, send, recv):
        def one(d, carry):
            u, device = chip_at(d)
            remote(data.at[u], landed.at[chip], send.at[d], recv.at[chip], device).start()
            return carry

        return one

    def collect(landed, send, recv):
        def one(d, carry):
            e = lax.rem(chip + d, 16)
            remote(landed.at[e], landed.at[e], send.at[d], recv.at[e], (z, op, y)).wait_recv()
            return carry

        lax.fori_loop(1, 16, one, 0)

    lax.fori_loop(1, 16, post(sink, rsink, bsend, br), 0)
    rsink[chip] = sink[chip]

    def step_one(n, carry):
        columns = win[source_at, :, :, pl.ds(pl.multiple_of(n * 256, 256), 256)].reshape(64, 256)
        first = dot(q0s[:, :64], columns).astype(BF16)
        v[:, n] = first.reshape(16, 32, 256)
        return carry

    lax.fori_loop(0, 16, step_one, 0, unroll=8)

    def step_two(b, carry):
        second = dot(v[b].reshape(512, 256), bd[b], NT)
        for n in range(16):
            for h in range(2):
                start = pl.multiple_of((b * 32 + n * 2 + h) * PITCH, 8)
                t2[pl.ds(start, 32), :] = second[n * 32:(n + 1) * 32, h * 128:(h + 1) * 128]
        return carry

    lax.fori_loop(0, 16, step_two, 0, unroll=8)

    def step_three(d, carry):
        u = chip_at(d)[0]
        left = t2[pl.ds(u, 512, stride=PITCH), :].astype(BF16)
        right = t2[pl.ds(u + 16, 512, stride=PITCH), :].astype(BF16)
        both = dot(q1r[...], jnp.concatenate([left, right], axis=1))
        even = both[:64, :128] + pltpu.roll(both[64:, :128], 64, 1)
        odd = pltpu.roll(both[:64, 128:], 64, 1) + both[64:, 128:]
        prod[u] = jnp.where(low, even, odd).astype(BF16)
        return carry

    for start in (1, 5, 9):
        lax.fori_loop(start, start + 4, step_three, 0, unroll=4)
        lax.fori_loop(start, start + 4, post(prod, rprod, asend, ar), 0)
    lax.fori_loop(13, 17, lambda d, carry: step_three(lax.rem(d, 16), carry), 0, unroll=4)
    lax.fori_loop(13, 16, post(prod, rprod, asend, ar), 0)
    rprod[chip] = prod[chip]

    collect(rsink, bsend, br)
    for i in range(16):
        t2[i * 72:i * 72 + 64, :] = rsink[i].astype(F32)
    for r in range(64):
        ks[:, r * 128:(r + 1) * 128] = t2[pl.ds(r, 16, stride=72), :].astype(BF16)
    collect(rprod, asend, ar)
    for j in range(16):
        t2[j * 72:j * 72 + 64, :] = rprod[j].astype(F32)
    lane16 = iota((16, 128), 1) < 64
    for t in range(32):
        a = t2[pl.ds(2 * t, 16, stride=72), :]
        b = t2[pl.ds(2 * t + 1, 16, stride=72), :]
        kp[:, t * 128:(t + 1) * 128] = jnp.where(lane16, a, pltpu.roll(b, 64, 1)).astype(BF16)
        kp[:, (32 + t) * 128:(33 + t) * 128] = jnp.where(lane16, pltpu.roll(a, 64, 1), b).astype(BF16)
    square = dot(ks[...], kp[...], NT)
    gl, gj = iota((16, 128), 0), iota((16, 128), 1)
    table = dot(square, jnp.where(gl == lax.rem(gj, 16), 1.0, 0.0).astype(F32), precision=lax.Precision.HIGHEST)
    mine = jnp.where(gj // 16 == lax.rem(gl, 8), table, 0.0)
    part[chip] = jnp.sum(mine.reshape(2, 8, 128), axis=1)

    def tell(d, carry):
        remote(part.at[chip], part.at[chip], rs.at[d], rr.at[chip], chip_at(d)[1]).start()
        return carry

    lax.fori_loop(1, 16, tell, 0)
    collect(part, rs, rr)
    core_part[c] = jnp.sum(part[...], axis=0)
    swap = remote(core_part.at[c], core_part.at[c], xs, xr, (z, other, y))
    swap.start()
    swap.wait_send()
    remote(core_part.at[1 - c], core_part.at[1 - c], xs, xr, (z, other, y)).wait_recv()
    out[...] = core_part[0] + core_part[1]

    for k in range(2):
        @pl.when(2 * c + k != y)
        def _(k=k):
            remote(elements.at[0, k], win.at[0, y], own_send.at[k], own_recv.at[k], (z, op, y)).wait_send()

        for way in range(2):
            for hop in range(1, (plus_hops, minus_hops)[way][k] + 1):
                along(0, hop, k, way).wait_send()
        for slot in range(zn):
            to_core(slot, k).wait_send()
    for d in range(1, 4):
        remote(qn.at[y], qn.at[y], qs.at[d], qr.at[d], (z, op, y)).wait_send()

    def left(d, carry):
        remote(sink.at[0], rsink.at[0], bsend.at[d], br.at[0], (z, op, y)).wait_send()
        remote(prod.at[0], rprod.at[0], asend.at[d], ar.at[0], (z, op, y)).wait_send()
        remote(part.at[0], part.at[0], rs.at[d], rr.at[0], (z, op, y)).wait_send()
        return carry

    lax.fori_loop(1, 16, left, 0)


def solution(mesh):
    zn = mesh.shape["tm"]

    def body(pairs, elements, perambs):
        dma = pltpu.SemaphoreType.DMA
        result = pl.pallas_call(
            functools.partial(kernel, zn),
            out_shape=jax.ShapeDtypeStruct((2, 128), F32),
            in_specs=[
                pl.BlockSpec(memory_space=pltpu.SMEM),
                pl.BlockSpec(memory_space=pl.ANY),
                pl.BlockSpec(memory_space=pl.ANY),
            ],
            out_specs=pl.BlockSpec(memory_space=pltpu.VMEM),
            scratch_shapes=[
                pltpu.VMEM((zn, 4, 16, 4096), BF16),
                pltpu.VMEM((16, 3, 4, 4096), BF16),
                pltpu.VMEM((256, 128), F32),
                pltpu.VMEM((64, 128), F32),
                pltpu.VMEM((4, 4, 3, 64, 128), BF16),
                pltpu.VMEM((512, 128), BF16),
                pltpu.VMEM((16, 256, 256), BF16),
                pltpu.VMEM((128, 512), BF16),
                pltpu.VMEM((16, 16, 32, 256), BF16),
                pltpu.VMEM((512 * PITCH, 128), F32),
                pltpu.VMEM((16, 64, 128), BF16),
                pltpu.VMEM((16, 64, 128), BF16),
                pltpu.VMEM((16, 64, 128), BF16),
                pltpu.VMEM((16, 64, 128), BF16),
                pltpu.VMEM((16, 8192), BF16),
                pltpu.VMEM((16, 8192), BF16),
                pltpu.VMEM((16, 2, 128), F32),
                pltpu.VMEM((2, 2, 128), F32),
                dma, dma((2,)), dma((2,)),
                dma((2, zn, 2)), dma((2, zn, 2)), dma((zn, 2)), dma((zn, 2)),
                dma((4,)), dma((4,)),
                dma((16,)), dma((16,)), dma((16,)), dma((16,)), dma((16,)), dma((16,)),
                dma, dma,
            ],
            compiler_params=pltpu.CompilerParams(
                collective_id=0, has_side_effects=True, vmem_limit_bytes=56 * 1024 * 1024
            ),
        )(pairs.T, elements, perambs.transpose(0, 2, 1, 3))
        return result.reshape(1, 16, 16)

    placed = (P(), P("tm", "op", "spin", None), P(None, "spin", None, None))
    return jax.shard_map(
        body, mesh=mesh, in_specs=placed, out_specs=P("tm", None, None), check_vma=False
    )
```

```python
import functools

import jax
import jax.numpy as jnp
from jax import lax
from jax.experimental import pallas as pl
from jax.experimental.pallas import tpu as pltpu
from jax.sharding import PartitionSpec as P

MESH = pl.DeviceIdType.MESH
F32 = jnp.float32
BF16 = jnp.bfloat16
NN = (((1,), (0,)), ((), ()))
NT = (((1,), (1,)), ((), ()))
PITCH = 40
REACH = 4
TRIES = ((1, 0), (-1, 0), (1, 8), (-1, 8))


def dot(a, b, dims=NN, precision=None):
    return lax.dot_general(a, b, dims, precision=precision, preferred_element_type=F32)


def iota(shape, axis):
    return lax.broadcasted_iota(jnp.int32, shape, axis)


def assign(zn, z, pairs):
    full = (1 << zn) - 1

    def window(centre, reach):
        mask = lax.shift_left(jnp.int32((1 << (2 * reach + 1)) - 1), lax.rem(centre + zn - reach, zn))
        return (mask | lax.shift_right_logical(mask, jnp.int32(zn))) & full

    found, early, late = jnp.int32(0), jnp.int32(-1), jnp.int32(-1)
    for sign, turn in TRIES:
        own = lax.shift_left(jnp.int32(1), lax.rem(sign * z + turn + zn, zn))

        def place(p, state, sign=sign, turn=turn, own=own):
            free_early, free_late, good, mine_early, mine_late = state
            source = lax.rem(sign * pairs[0, p] + turn + zn, zn)
            sink = lax.rem(sign * pairs[1, p] + turn + zn, zn)
            around = window(sink, REACH)
            near = window(source, 2) & around & free_early
            wide = window(source, REACH) & around & free_late
            at_early = near & -near
            at_late = jnp.where(near == 0, wide & -wide, 0)
            return (
                free_early - at_early,
                free_late - at_late,
                jnp.where((at_early | at_late) == 0, 0, good),
                jnp.where(at_early == own, p, mine_early),
                jnp.where(at_late == own, p, mine_late),
            )

        start = (jnp.int32(full), jnp.int32(full), jnp.int32(1), jnp.int32(-1), jnp.int32(-1))
        _, _, good, mine_early, mine_late = lax.fori_loop(0, zn, place, start, unroll=4)
        early = jnp.where(found == 1, early, mine_early)
        late = jnp.where(found == 1, late, mine_late)
        found = jnp.maximum(found, good)
    return found, early, late


def kernel(zn, whole, pairs, elements, perambs, out, *rest):
    if whole:
        flag, rest = None, rest
    else:
        flag, rest = rest[0], rest[1:]
    (near, far, pv, ps, s8, n64, qn, q0s, bd, q1r, v, t2, prod, sink, rprod, rsink, ks, kp, part, zpart, core_part,
     pv_sem, own_recv, own_send, zr, zs, cr, cs, qr, qs, ar, asend, br, bsend, rr, rs, wr, ws, xr, xs) = rest
    slots = 1 if whole else 2
    z, op, y = lax.axis_index("tm"), lax.axis_index("op"), lax.axis_index("spin")
    x, c = op // 2, lax.rem(op, 2)
    chip = x * 4 + y
    other = op + 1 - 2 * c
    up, down = lax.rem(z + 1, zn), lax.rem(z + zn - 1, zn)

    def remote(src, dst, send, recv, device):
        return pltpu.make_async_remote_copy(
            src_ref=src, dst_ref=dst, send_sem=send, recv_sem=recv, device_id=device, device_id_type=MESH
        )

    take_perambs = pltpu.make_async_copy(perambs, pv, pv_sem)
    take_perambs.start()

    barrier = pltpu.get_barrier_semaphore()

    def greet(i, carry):
        o, s = i // 4, lax.rem(i, 4)

        @pl.when(i != op * 4 + y)
        def _():
            pl.semaphore_signal(barrier, inc=1, device_id=(z, o, s), device_id_type=MESH)

        return carry

    lax.fori_loop(0, 32, greet, 0)
    if whole:
        for place in (up, down):
            pl.semaphore_signal(barrier, inc=1, device_id=(place, op, y), device_id_type=MESH)
        pl.semaphore_wait(barrier, 33)
    else:
        def greet_along(d, carry):
            pl.semaphore_signal(barrier, inc=1, device_id=(lax.rem(z + d, zn), op, y), device_id_type=MESH)
            return carry

        lax.fori_loop(1, zn, greet_along, 0)
        pl.semaphore_wait(barrier, 31 + zn - 1)

    odd_y = lax.rem(y, 2)
    for k in range(2):
        j = lax.rem(k + 1 - odd_y, 2)
        target = 2 * c + j

        @pl.when(target != y)
        def _(j=j, target=target):
            remote(
                elements.at[0, j], near.at[0, y], own_send.at[j], own_recv.at[odd_y], (z, 2 * x + y // 2, target)
            ).start()

        @pl.when(target == y)
        def _(j=j):
            pltpu.make_async_copy(elements.at[0, j], near.at[0, y], own_recv.at[odd_y]).start()

    apart = lax.rem(c + y // 2, 2)
    first_piece = lax.rem(odd_y + apart, 2)
    piece = [lax.rem(first_piece + k, 2) for k in range(2)]
    if whole:
        hops = ((zn // 2, zn // 2 - 1), (zn // 2 - 1, zn // 2))
        held = list(range(zn))
    else:
        hops = ((REACH, REACH), (REACH, REACH))
        held = list(range(REACH + 1)) + list(range(zn - REACH, zn))

    def slab(behind):
        if behind <= 2:
            return near.at[behind]
        if behind >= zn - 2:
            return near.at[behind - (zn - 5)]
        if whole or behind <= REACH:
            return far.at[behind - 3]
        return far.at[behind - 3 - (zn - 2 * REACH - 1)]

    def behind_of(way, hop):
        return hop if way == 0 else (zn - hop) % zn

    def to_core(behind, k):
        block = slab(behind).at[2 * c + k]
        return remote(block, block, cs.at[behind, k], cr.at[behind, k], (z, other, y))

    def from_core(behind, k):
        block = slab(behind).at[2 * (1 - c) + k]
        return remote(block, block, cs.at[behind, k], cr.at[behind, k], (z, other, y))

    def along(way, hop, k):
        return remote(
            slab(behind_of(way, hop - 1)).at[2 * c + k], slab(behind_of(way, hop)).at[2 * c + k],
            zs.at[way, hop, k], zr.at[way, hop, k], ((up, down)[way], op, y),
        )

    def hand_on(hop, turn):
        k = piece[turn]
        for way in range(2):
            if hop <= hops[way][turn]:
                if hop > 0:
                    along(way, hop, k).wait_recv()
                if hop < hops[way][turn]:
                    along(way, hop + 1, k).start()
                if hop > 0 or way == 0:
                    to_core(behind_of(way, hop), k).start()

    for turn in range(2):
        k = piece[turn]
        pltpu.make_async_copy(elements.at[0, k], near.at[0, 2 * c + k], own_recv.at[k]).wait()
        hand_on(0, turn)

    if whole:
        work = [z]
    else:
        found, early, late = assign(zn, z, pairs)
        flag[0] = found
        work = [jnp.maximum(early, 0), jnp.maximum(late, 0)]
    take_perambs.wait()
    for n in range(slots):
        ps[n, y] = pv[work[n]]
        for d in range(1, 4):
            remote(ps.at[n, y], ps.at[n, y], qs.at[n, d], qr.at[n, d], (z, op, lax.rem(y + d, 4))).start()
    lane = iota((32, 128), 1) < 64
    low = iota((64, 128), 1) < 64
    bd[...] = jnp.zeros_like(bd)

    def matrices(n):
        for d in range(1, 4):
            remote(
                ps.at[n, y], ps.at[n, lax.rem(y + 4 - d, 4)], qs.at[n, d], qr.at[n, d], (z, op, y)
            ).wait_recv()

        def flat(i, carry):
            g, l = i // 3, lax.rem(i, 3)
            rows = ps[n, g, l].astype(F32)
            for t in range(32):
                s8[t * 8:t * 8 + 4, :] = rows[:, t * 128:(t + 1) * 128]
            for b in range(4):
                q = s8[pl.ds(b, 32, stride=8), :]
                r = pltpu.roll(q, 64, 1)
                n64[pl.ds(b * 64, 32, stride=2), :] = jnp.where(lane, q, r)
                n64[pl.ds(b * 64 + 1, 32, stride=2), :] = jnp.where(lane, r, q)
                qn[g, b, l] = n64[b * 64:(b + 1) * 64, :].astype(BF16)
            return carry

        lax.fori_loop(0, 12, flat, 0)

        def blocks(b, carry):
            g, bb = b // 4, lax.rem(b, 4)
            q0s[pl.ds(b * 32, 32), :] = qn[g, bb, 0, pl.ds(32 * c, 32), :]
            q2 = qn[g, bb, 2]
            none = jnp.zeros_like(q2)
            for k in range(4):
                half = jnp.where(low, q2, none) if k % 2 == 0 else jnp.where(low, none, q2)
                bd[b, k * 64:(k + 1) * 64, (k // 2) * 128:(k // 2 + 1) * 128] = half
            return carry

        lax.fori_loop(0, 16, blocks, 0)
        row, column = iota((128, 128), 0), iota((128, 128), 1)
        for g in range(4):
            for lo in range(2):
                acc = jnp.zeros((64, 128), F32)
                for bb in range(4):
                    spot = (row < 64) & (lax.rem(row, 2) == lo) & (column == bb * 32 + row // 2)
                    acc += dot(qn[g, bb, 1], jnp.where(spot, 1.0, 0.0).astype(BF16))
                q1r[lo * 64:(lo + 1) * 64, g * 128:(g + 1) * 128] = acc.astype(BF16)

    def seek(time):
        behind = lax.rem(z + zn - time, zn)
        is_near = (behind <= 2) | (behind >= zn - 2)
        near_at = jnp.where(is_near, jnp.where(behind <= 2, behind, behind - (zn - 5)), 0)
        if whole:
            far_at = jnp.where(is_near, 0, behind - 3)
        else:
            far_at = jnp.where(behind <= REACH, behind - 3, behind - 3 - (zn - 2 * REACH - 1))
            far_at = jnp.clip(jnp.where(is_near, 0, far_at), 0, 2 * REACH - 5)
        return is_near, near_at, far_at

    def chip_at(d):
        xx, yy = lax.rem(x + d // 4, 4), lax.rem(y + lax.rem(d, 4), 4)
        return xx * 4 + yy, (z, 2 * xx + c, yy)

    def post(data, landed, send, recv):
        def one(d, carry):
            u, device = chip_at(d)
            remote(data.at[u], landed.at[chip], send.at[d], recv.at[chip], device).start()
            return carry

        return one

    def collect(landed, send, recv):
        def one(d, carry):
            e = lax.rem(chip + d, 16)
            remote(landed.at[e], landed.at[e], send.at[d], recv.at[e], (z, op, y)).wait_recv()
            return carry

        lax.fori_loop(1, 16, one, 0)

    def send_sink(n):
        is_near, near_at, far_at = seek(pairs[1, work[n]])
        for k in range(2):
            def lift(t, carry, k=k):
                columns = pl.ds(pl.multiple_of(t * 128, 128), 128)
                tile = jnp.where(is_near, near[near_at, 2 * c + k, :, columns].astype(F32),
                                 far[far_at, 2 * c + k, :, columns].astype(F32))
                t2[pl.ds(pl.multiple_of((k * 32 + t) * 24, 8), 16), :] = tile
                return carry

            lax.fori_loop(0, 32, lift, 0, unroll=8)

        def cut(u, carry):
            sink[n, u] = t2[pl.ds(u, 64, stride=24), :].astype(BF16)
            return carry

        lax.fori_loop(0, 16, cut, 0, unroll=8)
        lax.fori_loop(1, 16, post(sink.at[n], rsink.at[n], bsend.at[n], br.at[n]), 0)
        rsink[n, chip] = sink[n, chip]

    def step_one(n, only_near):
        is_near, near_at, far_at = seek(pairs[0, work[n]])

        def body(t, carry):
            columns = pl.ds(pl.multiple_of(t * 256, 256), 256)
            tile = near[near_at, :, :, columns]
            if not only_near:
                tile = jnp.where(is_near, tile.astype(F32), far[far_at, :, :, columns].astype(F32)).astype(BF16)
            first = dot(q0s[:, :64], tile.reshape(64, 256)).astype(BF16)
            v[:, t] = first.reshape(16, 32, 256)
            return carry

        lax.fori_loop(0, 16, body, 0, unroll=8)

    def step_two():
        def body(b, carry):
            second = dot(v[b].reshape(512, 256), bd[b], NT)
            for n in range(16):
                for h in range(2):
                    start = pl.multiple_of((b * 32 + n * 2 + h) * PITCH, 8)
                    t2[pl.ds(start, 32), :] = second[n * 32:(n + 1) * 32, h * 128:(h + 1) * 128]
            return carry

        lax.fori_loop(0, 16, body, 0, unroll=8)

    def step_three(n):
        def body(d, carry):
            u = chip_at(lax.rem(d, 16))[0]
            left = t2[pl.ds(u, 512, stride=PITCH), :].astype(BF16)
            right = t2[pl.ds(u + 16, 512, stride=PITCH), :].astype(BF16)
            both = dot(q1r[...], jnp.concatenate([left, right], axis=1))
            even = both[:64, :128] + pltpu.roll(both[64:, :128], 64, 1)
            odd = pltpu.roll(both[:64, 128:], 64, 1) + both[64:, 128:]
            prod[n, u] = jnp.where(low, even, odd).astype(BF16)
            return carry

        for start in (1, 5, 9, 13):
            lax.fori_loop(start, start + 4, body, 0, unroll=4)
            send = post(prod.at[n], rprod.at[n], asend.at[n], ar.at[n])
            lax.fori_loop(start, min(start + 4, 16), send, 0)
        rprod[n, chip] = prod[n, chip]

    if whole:
        for hop in range(1, max(hops[0]) + 1):
            for turn in range(2):
                hand_on(hop, turn)
            if hop == 1:
                matrices(0)
        for behind in held:
            for k in range(2):
                from_core(behind, k).wait_recv()
    else:
        for turn in range(2):
            hand_on(1, turn)
        matrices(0)
        for turn in range(2):
            hand_on(2, turn)
        close = [b for b in held if b <= 2 or b >= zn - 2]
        for behind in close:
            for k in range(2):
                from_core(behind, k).wait_recv()
        step_one(0, True)
        hand_on(3, 0)
        step_two()
        hand_on(3, 1)
        step_three(0)
        hand_on(4, 0)
        matrices(1)
        hand_on(4, 1)
        for behind in held:
            if behind not in close:
                for k in range(2):
                    from_core(behind, k).wait_recv()

    last = slots - 1
    for n in reversed(range(slots)):
        send_sink(n)
    step_one(last, False)
    step_two()
    step_three(last)

    lane16 = iota((16, 128), 1) < 64
    wl, wj = iota((16, 128), 0), iota((16, 128), 1)

    def contract(n):
        collect(rsink.at[n], bsend.at[n], br.at[n])
        for i in range(16):
            t2[i * 72:i * 72 + 64, :] = rsink[n, i].astype(F32)
        for r in range(64):
            ks[:, r * 128:(r + 1) * 128] = t2[pl.ds(r, 16, stride=72), :].astype(BF16)
        collect(rprod.at[n], asend.at[n], ar.at[n])
        for j in range(16):
            t2[j * 72:j * 72 + 64, :] = rprod[n, j].astype(F32)
        for t in range(32):
            a = t2[pl.ds(2 * t, 16, stride=72), :]
            b = t2[pl.ds(2 * t + 1, 16, stride=72), :]
            kp[:, t * 128:(t + 1) * 128] = jnp.where(lane16, a, pltpu.roll(b, 64, 1)).astype(BF16)
            kp[:, (32 + t) * 128:(33 + t) * 128] = jnp.where(lane16, pltpu.roll(a, 64, 1), b).astype(BF16)
        square = dot(ks[...], kp[...], NT)
        table = dot(square, jnp.where(wl == lax.rem(wj, 16), 1.0, 0.0).astype(F32), precision=lax.Precision.HIGHEST)
        mine = jnp.where(wj // 16 == lax.rem(wl, 8), table, 0.0)
        return jnp.sum(mine.reshape(2, 8, 128), axis=1)

    tables = [contract(n) for n in range(slots)]
    if whole:
        part[chip] = tables[0]
    else:
        for d in range(zn):
            p = lax.rem(z + d, zn)
            zpart[1, d] = jnp.where(early == p, tables[0], 0.0) + jnp.where(late == p, tables[1], 0.0)
            if d > 0:
                remote(zpart.at[1, d], zpart.at[0, d], ws.at[d], wr.at[d], (p, op, y)).start()
        zpart[0, 0] = zpart[1, 0]
        for d in range(1, zn):
            remote(zpart.at[1, d], zpart.at[0, d], ws.at[d], wr.at[d], (z, op, y)).wait_recv()
        part[chip] = jnp.sum(zpart[0], axis=0)

    def tell(d, carry):
        remote(part.at[chip], part.at[chip], rs.at[d], rr.at[chip], chip_at(d)[1]).start()
        return carry

    lax.fori_loop(1, 16, tell, 0)
    collect(part, rs, rr)
    core_part[c] = jnp.sum(part[...], axis=0)
    swap = remote(core_part.at[c], core_part.at[c], xs, xr, (z, other, y))
    swap.start()
    swap.wait_send()
    remote(core_part.at[1 - c], core_part.at[1 - c], xs, xr, (z, other, y)).wait_recv()
    out[...] = core_part[0] + core_part[1]

    for k in range(2):
        @pl.when(2 * c + k != y)
        def _(k=k):
            remote(elements.at[0, k], near.at[0, y], own_send.at[k], own_recv.at[k], (z, op, y)).wait_send()

        for way in range(2):
            for hop in range(1, hops[way][k] + 1):
                along(way, hop, piece[k]).wait_send()
        for behind in held:
            to_core(behind, k).wait_send()
    for n in range(slots):
        for d in range(1, 4):
            remote(ps.at[n, y], ps.at[n, y], qs.at[n, d], qr.at[n, d], (z, op, y)).wait_send()

        def left(d, carry, n=n):
            remote(sink.at[n, 0], rsink.at[n, 0], bsend.at[n, d], br.at[n, 0], (z, op, y)).wait_send()
            remote(prod.at[n, 0], rprod.at[n, 0], asend.at[n, d], ar.at[n, 0], (z, op, y)).wait_send()
            return carry

        lax.fori_loop(1, 16, left, 0)

    def left_tables(d, carry):
        remote(part.at[0], part.at[0], rs.at[d], rr.at[0], (z, op, y)).wait_send()
        return carry

    lax.fori_loop(1, 16, left_tables, 0)
    if not whole:
        for d in range(1, zn):
            remote(zpart.at[1, d], zpart.at[0, d], ws.at[d], wr.at[d], (z, op, y)).wait_send()


def call(zn, whole, pairs, elements, perambs):
    dma = pltpu.SemaphoreType.DMA
    slots = 1 if whole else 2
    far = zn - 5 if whole else 2 * REACH - 4
    out_shape = [jax.ShapeDtypeStruct((2, 128), F32)]
    out_specs = [pl.BlockSpec(memory_space=pltpu.VMEM)]
    if not whole:
        out_shape.append(jax.ShapeDtypeStruct((1,), jnp.int32))
        out_specs.append(pl.BlockSpec(memory_space=pltpu.SMEM))
    return pl.pallas_call(
        functools.partial(kernel, zn, whole),
        out_shape=out_shape,
        in_specs=[
            pl.BlockSpec(memory_space=pltpu.SMEM),
            pl.BlockSpec(memory_space=pl.ANY),
            pl.BlockSpec(memory_space=pl.ANY),
        ],
        out_specs=out_specs,
        scratch_shapes=[
            pltpu.VMEM((5, 4, 16, 4096), BF16),
            pltpu.VMEM((far, 4, 16, 4096), BF16),
            pltpu.VMEM((16, 3, 4, 4096), BF16),
            pltpu.VMEM((slots, 4, 3, 4, 4096), BF16),
            pltpu.VMEM((256, 128), F32),
            pltpu.VMEM((256, 128), F32),
            pltpu.VMEM((4, 4, 3, 64, 128), BF16),
            pltpu.VMEM((512, 128), BF16),
            pltpu.VMEM((16, 256, 256), BF16),
            pltpu.VMEM((128, 512), BF16),
            pltpu.VMEM((16, 16, 32, 256), BF16),
            pltpu.VMEM((512 * PITCH, 128), F32),
            pltpu.VMEM((slots, 16, 64, 128), BF16),
            pltpu.VMEM((slots, 16, 64, 128), BF16),
            pltpu.VMEM((slots, 16, 64, 128), BF16),
            pltpu.VMEM((slots, 16, 64, 128), BF16),
            pltpu.VMEM((16, 8192), BF16),
            pltpu.VMEM((16, 8192), BF16),
            pltpu.VMEM((16, 2, 128), F32),
            pltpu.VMEM((2, zn, 2, 128), F32),
            pltpu.VMEM((2, 2, 128), F32),
            dma, dma((2,)), dma((2,)),
            dma((2, zn, 2)), dma((2, zn, 2)), dma((zn, 2)), dma((zn, 2)),
            dma((slots, 4)), dma((slots, 4)),
            dma((slots, 16)), dma((slots, 16)), dma((slots, 16)), dma((slots, 16)), dma((16,)), dma((16,)),
            dma((zn,)), dma((zn,)), dma, dma,
        ],
        compiler_params=pltpu.CompilerParams(
            collective_id=1 if whole else 0, has_side_effects=True, vmem_limit_bytes=56 * 1024 * 1024
        ),
    )(pairs, elements, perambs)


def solution(mesh):
    zn = mesh.shape["tm"]

    def body(pairs, elements, perambs):
        given = (pairs.T, elements, perambs.transpose(0, 2, 1, 3))
        table = call(zn, True, *given)[0]
        return table.reshape(1, 16, 16)

    placed = (P(), P("tm", "op", "spin", None), P(None, "spin", None, None))
    return jax.shard_map(
        body, mesh=mesh, in_specs=placed, out_specs=P("tm", None, None), check_vma=False
    )
```

```python
import functools

import jax
import jax.numpy as jnp
from jax import lax
from jax.experimental import pallas as pl
from jax.experimental.pallas import tpu as pltpu
from jax.sharding import PartitionSpec as P

MESH = pl.DeviceIdType.MESH
F32 = jnp.float32
BF16 = jnp.bfloat16
NN = (((1,), (0,)), ((), ()))
NT = (((1,), (1,)), ((), ()))
PITCH = 40
REACH = 4
TRIES = ((1, 0), (-1, 0), (1, 8), (-1, 8))


def dot(a, b, dims=NN, precision=None):
    return lax.dot_general(a, b, dims, precision=precision, preferred_element_type=F32)


def iota(shape, axis):
    return lax.broadcasted_iota(jnp.int32, shape, axis)


def assign(zn, z, pairs):
    full = (1 << zn) - 1

    def window(centre, reach):
        mask = lax.shift_left(jnp.int32((1 << (2 * reach + 1)) - 1), lax.rem(centre + zn - reach, zn))
        return (mask | lax.shift_right_logical(mask, jnp.int32(zn))) & full

    found, early, late = jnp.int32(0), jnp.int32(-1), jnp.int32(-1)
    for sign, turn in TRIES:
        own = lax.shift_left(jnp.int32(1), lax.rem(sign * z + turn + zn, zn))

        def place(p, state, sign=sign, turn=turn, own=own):
            free_early, free_late, good, mine_early, mine_late = state
            source = lax.rem(sign * pairs[0, p] + turn + zn, zn)
            sink = lax.rem(sign * pairs[1, p] + turn + zn, zn)
            around = window(sink, REACH)
            near = window(source, 2) & around & free_early
            wide = window(source, REACH) & around & free_late
            at_early = near & -near
            at_late = jnp.where(near == 0, wide & -wide, 0)
            return (
                free_early - at_early,
                free_late - at_late,
                jnp.where((at_early | at_late) == 0, 0, good),
                jnp.where(at_early == own, p, mine_early),
                jnp.where(at_late == own, p, mine_late),
            )

        start = (jnp.int32(full), jnp.int32(full), jnp.int32(1), jnp.int32(-1), jnp.int32(-1))
        _, _, good, mine_early, mine_late = lax.fori_loop(0, zn, place, start, unroll=4)
        early = jnp.where(found == 1, early, mine_early)
        late = jnp.where(found == 1, late, mine_late)
        found = jnp.maximum(found, good)
    return found, early, late


def kernel(zn, whole, pairs, elements, perambs, out, *rest):
    if whole:
        flag, rest = None, rest
    else:
        flag, rest = rest[0], rest[1:]
    slots = 1 if whole else 2
    own, rest = rest[:5 * slots], rest[5 * slots:]
    ps, prod, sink, rprod, rsink = (own[i * slots:(i + 1) * slots] for i in range(5))
    (near, far, pv, s8, n64, qn, q0s, bd, q1r, v, t2, ks, kp, part, zout, zin, core_part,
     pv_sem, own_recv, own_send, zr, zs, cr, cs, qr, qs, ar, asend, br, bsend, rr, rs, wr, ws, xr, xs) = rest
    z, op, y = lax.axis_index("tm"), lax.axis_index("op"), lax.axis_index("spin")
    x, c = op // 2, lax.rem(op, 2)
    chip = x * 4 + y
    other = op + 1 - 2 * c
    up, down = lax.rem(z + 1, zn), lax.rem(z + zn - 1, zn)

    def remote(src, dst, send, recv, device):
        return pltpu.make_async_remote_copy(
            src_ref=src, dst_ref=dst, send_sem=send, recv_sem=recv, device_id=device, device_id_type=MESH
        )

    take_perambs = pltpu.make_async_copy(perambs, pv, pv_sem)
    take_perambs.start()

    barrier = pltpu.get_barrier_semaphore()

    def greet(i, carry):
        o, s = i // 4, lax.rem(i, 4)

        @pl.when(i != op * 4 + y)
        def _():
            pl.semaphore_signal(barrier, inc=1, device_id=(z, o, s), device_id_type=MESH)

        return carry

    lax.fori_loop(0, 32, greet, 0)
    if whole:
        for place in (up, down):
            pl.semaphore_signal(barrier, inc=1, device_id=(place, op, y), device_id_type=MESH)
        pl.semaphore_wait(barrier, 33)
    else:
        def greet_along(d, carry):
            pl.semaphore_signal(barrier, inc=1, device_id=(lax.rem(z + d, zn), op, y), device_id_type=MESH)
            return carry

        lax.fori_loop(1, zn, greet_along, 0)
        pl.semaphore_wait(barrier, 31 + zn - 1)

    odd_y = lax.rem(y, 2)
    for k in range(2):
        j = lax.rem(k + 1 - odd_y, 2)
        target = 2 * c + j

        @pl.when(target != y)
        def _(j=j, target=target):
            remote(
                elements.at[0, j], near.at[0, y], own_send.at[j], own_recv.at[odd_y], (z, 2 * x + y // 2, target)
            ).start()

        @pl.when(target == y)
        def _(j=j):
            pltpu.make_async_copy(elements.at[0, j], near.at[0, y], own_recv.at[odd_y]).start()

    apart = lax.rem(c + y // 2, 2)
    first_piece = lax.rem(odd_y + apart, 2)
    piece = [lax.rem(first_piece + k, 2) for k in range(2)]
    if whole:
        hops = ((zn // 2, zn // 2 - 1), (zn // 2 - 1, zn // 2))
        held = list(range(zn))
    else:
        hops = ((REACH, REACH), (REACH, REACH))
        held = list(range(REACH + 1)) + list(range(zn - REACH, zn))

    def slab(behind):
        if behind <= 2:
            return near.at[behind]
        if behind >= zn - 2:
            return near.at[behind - (zn - 5)]
        if whole or behind <= REACH:
            return far.at[behind - 3]
        return far.at[behind - 3 - (zn - 2 * REACH - 1)]

    def behind_of(way, hop):
        return hop if way == 0 else (zn - hop) % zn

    def to_core(behind, k):
        block = slab(behind).at[2 * c + k]
        return remote(block, block, cs.at[behind, k], cr.at[behind, k], (z, other, y))

    def from_core(behind, k):
        block = slab(behind).at[2 * (1 - c) + k]
        return remote(block, block, cs.at[behind, k], cr.at[behind, k], (z, other, y))

    def along(way, hop, k):
        return remote(
            slab(behind_of(way, hop - 1)).at[2 * c + k], slab(behind_of(way, hop)).at[2 * c + k],
            zs.at[way, hop, k], zr.at[way, hop, k], ((up, down)[way], op, y),
        )

    def hand_on(hop, turn):
        k = piece[turn]
        for way in range(2):
            if hop <= hops[way][turn]:
                if hop > 0:
                    along(way, hop, k).wait_recv()
                if hop < hops[way][turn]:
                    along(way, hop + 1, k).start()
                if hop > 0 or way == 0:
                    to_core(behind_of(way, hop), k).start()

    for turn in range(2):
        k = piece[turn]
        pltpu.make_async_copy(elements.at[0, k], near.at[0, 2 * c + k], own_recv.at[k]).wait()
        hand_on(0, turn)

    if whole:
        work = [z]
    else:
        found, early, late = assign(zn, z, pairs)
        flag[0] = found
        work = [jnp.maximum(early, 0), jnp.maximum(late, 0)]
    take_perambs.wait()
    for n in range(slots):
        ps[n][y] = pv[work[n]]
        for d in range(1, 4):
            remote(ps[n].at[y], ps[n].at[y], qs.at[n, d], qr.at[n, d], (z, op, lax.rem(y + d, 4))).start()
    lane = iota((32, 128), 1) < 64
    low = iota((64, 128), 1) < 64
    bd[...] = jnp.zeros_like(bd)

    def matrices(n):
        for d in range(1, 4):
            remote(
                ps[n].at[y], ps[n].at[lax.rem(y + 4 - d, 4)], qs.at[n, d], qr.at[n, d], (z, op, y)
            ).wait_recv()

        def flat(l, carry, g):
            rows = ps[n][g, l].astype(F32)
            for t in range(32):
                s8[t * 8:t * 8 + 4, :] = rows[:, t * 128:(t + 1) * 128]
            for b in range(4):
                q = s8[pl.ds(b, 32, stride=8), :]
                r = pltpu.roll(q, 64, 1)
                n64[pl.ds(b * 64, 32, stride=2), :] = jnp.where(lane, q, r)
                n64[pl.ds(b * 64 + 1, 32, stride=2), :] = jnp.where(lane, r, q)
                qn[g, b, l] = n64[b * 64:(b + 1) * 64, :].astype(BF16)
            return carry

        for g in range(4):
            lax.fori_loop(0, 3, functools.partial(flat, g=g), 0)

        def blocks(b, carry):
            g, bb = b // 4, lax.rem(b, 4)
            q0s[pl.ds(b * 32, 32), :] = qn[g, bb, 0, pl.ds(32 * c, 32), :]
            q2 = qn[g, bb, 2]
            none = jnp.zeros_like(q2)
            for k in range(4):
                half = jnp.where(low, q2, none) if k % 2 == 0 else jnp.where(low, none, q2)
                bd[b, k * 64:(k + 1) * 64, (k // 2) * 128:(k // 2 + 1) * 128] = half
            return carry

        lax.fori_loop(0, 16, blocks, 0)
        row, column = iota((128, 128), 0), iota((128, 128), 1)
        for g in range(4):
            for lo in range(2):
                acc = jnp.zeros((64, 128), F32)
                for bb in range(4):
                    spot = (row < 64) & (lax.rem(row, 2) == lo) & (column == bb * 32 + row // 2)
                    acc += dot(qn[g, bb, 1], jnp.where(spot, 1.0, 0.0).astype(BF16))
                q1r[lo * 64:(lo + 1) * 64, g * 128:(g + 1) * 128] = acc.astype(BF16)

    def seek(time):
        behind = lax.rem(z + zn - time, zn)
        is_near = (behind <= 2) | (behind >= zn - 2)
        near_at = jnp.where(is_near, jnp.where(behind <= 2, behind, behind - (zn - 5)), 0)
        if whole:
            far_at = jnp.where(is_near, 0, behind - 3)
        else:
            far_at = jnp.where(behind <= REACH, behind - 3, behind - 3 - (zn - 2 * REACH - 1))
            far_at = jnp.clip(jnp.where(is_near, 0, far_at), 0, 2 * REACH - 5)
        return is_near, near_at, far_at

    def chip_at(d):
        xx, yy = lax.rem(x + d // 4, 4), lax.rem(y + lax.rem(d, 4), 4)
        return xx * 4 + yy, (z, 2 * xx + c, yy)

    def post(data, landed, send, recv):
        def one(d, carry):
            u, device = chip_at(d)
            remote(data.at[u], landed.at[chip], send.at[d], recv.at[chip], device).start()
            return carry

        return one

    def collect(landed, send, recv):
        def one(d, carry):
            e = lax.rem(chip + d, 16)
            remote(landed.at[e], landed.at[e], send.at[d], recv.at[e], (z, op, y)).wait_recv()
            return carry

        lax.fori_loop(1, 16, one, 0)

    def send_sink(n):
        is_near, near_at, far_at = seek(pairs[1, work[n]])
        for k in range(2):
            def lift(t, carry, k=k):
                columns = pl.ds(pl.multiple_of(t * 128, 128), 128)
                tile = jnp.where(is_near, near[near_at, 2 * c + k, :, columns].astype(F32),
                                 far[far_at, 2 * c + k, :, columns].astype(F32))
                t2[pl.ds(pl.multiple_of((k * 32 + t) * 24, 8), 16), :] = tile
                return carry

            lax.fori_loop(0, 32, lift, 0, unroll=8)

        def cut(u, carry):
            sink[n][u] = t2[pl.ds(u, 64, stride=24), :].astype(BF16)
            return carry

        lax.fori_loop(0, 16, cut, 0, unroll=8)
        lax.fori_loop(1, 16, post(sink[n], rsink[n], bsend.at[n], br.at[n]), 0)
        rsink[n][chip] = sink[n][chip]

    def step_one(n, only_near):
        is_near, near_at, far_at = seek(pairs[0, work[n]])

        def body(t, carry):
            columns = pl.ds(pl.multiple_of(t * 256, 256), 256)
            tile = near[near_at, :, :, columns]
            if not only_near:
                tile = jnp.where(is_near, tile.astype(F32), far[far_at, :, :, columns].astype(F32)).astype(BF16)
            first = dot(q0s[:, :64], tile.reshape(64, 256)).astype(BF16)
            v[:, t] = first.reshape(16, 32, 256)
            return carry

        lax.fori_loop(0, 16, body, 0, unroll=8)

    def step_two():
        def body(b, carry):
            second = dot(v[b].reshape(512, 256), bd[b], NT)
            for n in range(16):
                for h in range(2):
                    start = pl.multiple_of((b * 32 + n * 2 + h) * PITCH, 8)
                    t2[pl.ds(start, 32), :] = second[n * 32:(n + 1) * 32, h * 128:(h + 1) * 128]
            return carry

        lax.fori_loop(0, 16, body, 0, unroll=8)

    def step_three(n):
        def body(d, carry):
            u = chip_at(lax.rem(d, 16))[0]
            left = t2[pl.ds(u, 512, stride=PITCH), :].astype(BF16)
            right = t2[pl.ds(u + 16, 512, stride=PITCH), :].astype(BF16)
            both = dot(q1r[...], jnp.concatenate([left, right], axis=1))
            even = both[:64, :128] + pltpu.roll(both[64:, :128], 64, 1)
            odd = pltpu.roll(both[:64, 128:], 64, 1) + both[64:, 128:]
            prod[n][u] = jnp.where(low, even, odd).astype(BF16)
            return carry

        for start in (1, 5, 9, 13):
            lax.fori_loop(start, start + 4, body, 0, unroll=4)
            send = post(prod[n], rprod[n], asend.at[n], ar.at[n])
            lax.fori_loop(start, min(start + 4, 16), send, 0)
        rprod[n][chip] = prod[n][chip]

    if whole:
        for hop in range(1, max(hops[0]) + 1):
            for turn in range(2):
                hand_on(hop, turn)
            if hop == 1:
                matrices(0)
        for behind in held:
            for k in range(2):
                from_core(behind, k).wait_recv()
    else:
        for turn in range(2):
            hand_on(1, turn)
        matrices(0)
        for turn in range(2):
            hand_on(2, turn)
        close = [b for b in held if b <= 2 or b >= zn - 2]
        for behind in close:
            for k in range(2):
                from_core(behind, k).wait_recv()
        step_one(0, True)
        hand_on(3, 0)
        step_two()
        hand_on(3, 1)
        step_three(0)
        hand_on(4, 0)
        matrices(1)
        hand_on(4, 1)
        for behind in held:
            if behind not in close:
                for k in range(2):
                    from_core(behind, k).wait_recv()

    last = slots - 1
    for n in reversed(range(slots)):
        send_sink(n)
    step_one(last, False)
    step_two()
    step_three(last)

    lane16 = iota((16, 128), 1) < 64
    wl, wj = iota((16, 128), 0), iota((16, 128), 1)

    def contract(n):
        collect(rsink[n], bsend.at[n], br.at[n])
        for i in range(16):
            t2[i * 72:i * 72 + 64, :] = rsink[n][i].astype(F32)
        for r in range(64):
            ks[:, r * 128:(r + 1) * 128] = t2[pl.ds(r, 16, stride=72), :].astype(BF16)
        collect(rprod[n], asend.at[n], ar.at[n])
        for j in range(16):
            t2[j * 72:j * 72 + 64, :] = rprod[n][j].astype(F32)
        for t in range(32):
            a = t2[pl.ds(2 * t, 16, stride=72), :]
            b = t2[pl.ds(2 * t + 1, 16, stride=72), :]
            kp[:, t * 128:(t + 1) * 128] = jnp.where(lane16, a, pltpu.roll(b, 64, 1)).astype(BF16)
            kp[:, (32 + t) * 128:(33 + t) * 128] = jnp.where(lane16, pltpu.roll(a, 64, 1), b).astype(BF16)
        square = dot(ks[...], kp[...], NT)
        table = dot(square, jnp.where(wl == lax.rem(wj, 16), 1.0, 0.0).astype(F32), precision=lax.Precision.HIGHEST)
        mine = jnp.where(wj // 16 == lax.rem(wl, 8), table, 0.0)
        return jnp.sum(mine.reshape(2, 8, 128), axis=1)

    tables = [contract(n) for n in range(slots)]
    if whole:
        part[chip] = tables[0]
    else:
        for d in range(zn):
            p = lax.rem(z + d, zn)
            zout[d] = jnp.where(early == p, tables[0], 0.0) + jnp.where(late == p, tables[1], 0.0)
            if d > 0:
                remote(zout.at[d], zin.at[d], ws.at[d], wr.at[d], (p, op, y)).start()
        zin[0] = zout[0]
        for d in range(1, zn):
            remote(zout.at[d], zin.at[d], ws.at[d], wr.at[d], (z, op, y)).wait_recv()
        part[chip] = jnp.sum(zin[...], axis=0)

    def tell(d, carry):
        remote(part.at[chip], part.at[chip], rs.at[d], rr.at[chip], chip_at(d)[1]).start()
        return carry

    lax.fori_loop(1, 16, tell, 0)
    collect(part, rs, rr)
    core_part[c] = jnp.sum(part[...], axis=0)
    swap = remote(core_part.at[c], core_part.at[c], xs, xr, (z, other, y))
    swap.start()
    swap.wait_send()
    remote(core_part.at[1 - c], core_part.at[1 - c], xs, xr, (z, other, y)).wait_recv()
    out[...] = core_part[0] + core_part[1]

    for k in range(2):
        @pl.when(2 * c + k != y)
        def _(k=k):
            remote(elements.at[0, k], near.at[0, y], own_send.at[k], own_recv.at[k], (z, op, y)).wait_send()

        for way in range(2):
            for hop in range(1, hops[way][k] + 1):
                along(way, hop, piece[k]).wait_send()
        for behind in held:
            to_core(behind, k).wait_send()
    for n in range(slots):
        for d in range(1, 4):
            remote(ps[n].at[y], ps[n].at[y], qs.at[n, d], qr.at[n, d], (z, op, y)).wait_send()

        def left(d, carry, n=n):
            remote(sink[n].at[0], rsink[n].at[0], bsend.at[n, d], br.at[n, 0], (z, op, y)).wait_send()
            remote(prod[n].at[0], rprod[n].at[0], asend.at[n, d], ar.at[n, 0], (z, op, y)).wait_send()
            return carry

        lax.fori_loop(1, 16, left, 0)

    def left_tables(d, carry):
        remote(part.at[0], part.at[0], rs.at[d], rr.at[0], (z, op, y)).wait_send()
        return carry

    lax.fori_loop(1, 16, left_tables, 0)
    if not whole:
        for d in range(1, zn):
            remote(zout.at[d], zin.at[d], ws.at[d], wr.at[d], (z, op, y)).wait_send()


def call(zn, whole, pairs, elements, perambs):
    dma = pltpu.SemaphoreType.DMA
    slots = 1 if whole else 2
    far = zn - 5 if whole else 2 * REACH - 4
    out_shape = [jax.ShapeDtypeStruct((2, 128), F32)]
    out_specs = [pl.BlockSpec(memory_space=pltpu.VMEM)]
    if not whole:
        out_shape.append(jax.ShapeDtypeStruct((1,), jnp.int32))
        out_specs.append(pl.BlockSpec(memory_space=pltpu.SMEM))
    return pl.pallas_call(
        functools.partial(kernel, zn, whole),
        out_shape=out_shape,
        in_specs=[
            pl.BlockSpec(memory_space=pltpu.SMEM),
            pl.BlockSpec(memory_space=pl.ANY),
            pl.BlockSpec(memory_space=pl.ANY),
        ],
        out_specs=out_specs,
        scratch_shapes=[
            *[pltpu.VMEM((4, 3, 4, 4096), BF16)] * slots,
            *[pltpu.VMEM((16, 64, 128), BF16)] * (4 * slots),
            pltpu.VMEM((5, 4, 16, 4096), BF16),
            pltpu.VMEM((far, 4, 16, 4096), BF16),
            pltpu.VMEM((16, 3, 4, 4096), BF16),
            pltpu.VMEM((256, 128), F32),
            pltpu.VMEM((256, 128), F32),
            pltpu.VMEM((4, 4, 3, 64, 128), BF16),
            pltpu.VMEM((512, 128), BF16),
            pltpu.VMEM((16, 256, 256), BF16),
            pltpu.VMEM((128, 512), BF16),
            pltpu.VMEM((16, 16, 32, 256), BF16),
            pltpu.VMEM((512 * PITCH, 128), F32),
            pltpu.VMEM((16, 8192), BF16),
            pltpu.VMEM((16, 8192), BF16),
            pltpu.VMEM((16, 2, 128), F32),
            pltpu.VMEM((zn, 2, 128), F32),
            pltpu.VMEM((zn, 2, 128), F32),
            pltpu.VMEM((2, 2, 128), F32),
            dma, dma((2,)), dma((2,)),
            dma((2, zn, 2)), dma((2, zn, 2)), dma((zn, 2)), dma((zn, 2)),
            dma((slots, 4)), dma((slots, 4)),
            dma((slots, 16)), dma((slots, 16)), dma((slots, 16)), dma((slots, 16)), dma((16,)), dma((16,)),
            dma((zn,)), dma((zn,)), dma, dma,
        ],
        compiler_params=pltpu.CompilerParams(
            collective_id=1 if whole else 0, has_side_effects=True, vmem_limit_bytes=56 * 1024 * 1024
        ),
    )(pairs, elements, perambs)


def solution(mesh):
    zn = mesh.shape["tm"]

    def body(pairs, elements, perambs):
        given = (pairs.T, elements, perambs.transpose(0, 2, 1, 3))
        table, found = call(zn, False, *given)
        table = lax.cond(found[0] == 1, lambda: table, lambda: call(zn, True, *given)[0])
        return table.reshape(1, 16, 16)

    placed = (P(), P("tm", "op", "spin", None), P(None, "spin", None, None))
    return jax.shard_map(
        body, mesh=mesh, in_specs=placed, out_specs=P("tm", None, None), check_vma=False
    )
```

```python
import functools

import jax
import jax.numpy as jnp
from jax import lax
from jax.experimental import pallas as pl
from jax.experimental.pallas import tpu as pltpu
from jax.sharding import PartitionSpec as P

MESH = pl.DeviceIdType.MESH
F32 = jnp.float32
BF16 = jnp.bfloat16
NN = (((1,), (0,)), ((), ()))
NT = (((1,), (1,)), ((), ()))
PITCH = 40
REACH = 4
TRIES = ((1, 0), (-1, 0), (1, 8), (-1, 8))


def dot(a, b, dims=NN, precision=None):
    return lax.dot_general(a, b, dims, precision=precision, preferred_element_type=F32)


def iota(shape, axis):
    return lax.broadcasted_iota(jnp.int32, shape, axis)


def assign(zn, z, pairs):
    full = (1 << zn) - 1

    def window(centre, reach):
        mask = lax.shift_left(jnp.int32((1 << (2 * reach + 1)) - 1), lax.rem(centre + zn - reach, zn))
        return (mask | lax.shift_right_logical(mask, jnp.int32(zn))) & full

    found, early, late = jnp.int32(0), jnp.int32(-1), jnp.int32(-1)
    for sign, turn in TRIES:
        own = lax.shift_left(jnp.int32(1), lax.rem(sign * z + turn + zn, zn))

        def place(p, state, sign=sign, turn=turn, own=own):
            free_early, free_late, good, mine_early, mine_late = state
            source = lax.rem(sign * pairs[0, p] + turn + zn, zn)
            sink = lax.rem(sign * pairs[1, p] + turn + zn, zn)
            around = window(sink, REACH)
            near = window(source, 2) & around & free_early
            wide = window(source, REACH) & around & free_late
            at_early = near & -near
            at_late = jnp.where(near == 0, wide & -wide, 0)
            return (
                free_early - at_early,
                free_late - at_late,
                jnp.where((at_early | at_late) == 0, 0, good),
                jnp.where(at_early == own, p, mine_early),
                jnp.where(at_late == own, p, mine_late),
            )

        start = (jnp.int32(full), jnp.int32(full), jnp.int32(1), jnp.int32(-1), jnp.int32(-1))
        _, _, good, mine_early, mine_late = lax.fori_loop(0, zn, place, start, unroll=4)
        early = jnp.where(found == 1, early, mine_early)
        late = jnp.where(found == 1, late, mine_late)
        found = jnp.maximum(found, good)
    return found, early, late


def kernel(zn, whole, pairs, elements, perambs, out, *rest):
    if whole:
        flag, rest = None, rest
    else:
        flag, rest = rest[0], rest[1:]
    slots = 1 if whole else 2
    own, rest = rest[:5 * slots], rest[5 * slots:]
    ps, prod, sink, rprod, rsink = (own[i * slots:(i + 1) * slots] for i in range(5))
    (near, far, pv, s8, n64, qn, q0s, bd, q1r, v, t2, ks, kp, part, zout, zin,
     pv_sem, own_recv, own_send, zr, zs, cr, cs, qr, qs, ar, asend, br, bsend, rr, rs, wr, ws, token) = rest
    z, op, y = lax.axis_index("tm"), lax.axis_index("op"), lax.axis_index("spin")
    x, c = op // 2, lax.rem(op, 2)
    chip = x * 4 + y
    other = op + 1 - 2 * c
    up, down = lax.rem(z + 1, zn), lax.rem(z + zn - 1, zn)

    def remote(src, dst, send, recv, device):
        return pltpu.make_async_remote_copy(
            src_ref=src, dst_ref=dst, send_sem=send, recv_sem=recv, device_id=device, device_id_type=MESH
        )

    take_perambs = pltpu.make_async_copy(perambs, pv, pv_sem)
    take_perambs.start()

    barrier = pltpu.get_barrier_semaphore()

    def greet(i, carry):
        o, s = i // 4, lax.rem(i, 4)

        @pl.when(i != op * 4 + y)
        def _():
            pl.semaphore_signal(barrier, inc=1, device_id=(z, o, s), device_id_type=MESH)

        return carry

    lax.fori_loop(0, 32, greet, 0)
    for place in (up, down):
        pl.semaphore_signal(barrier, inc=1, device_id=(place, op, y), device_id_type=MESH)
    pl.semaphore_wait(barrier, 33)

    odd_y = lax.rem(y, 2)
    for k in range(2):
        j = lax.rem(k + 1 - odd_y, 2)
        target = 2 * c + j

        @pl.when(target != y)
        def _(j=j, target=target):
            remote(
                elements.at[0, j], near.at[0, y], own_send.at[j], own_recv.at[odd_y], (z, 2 * x + y // 2, target)
            ).start()

        @pl.when(target == y)
        def _(j=j):
            pltpu.make_async_copy(elements.at[0, j], near.at[0, y], own_recv.at[odd_y]).start()

    apart = lax.rem(c + y // 2, 2)
    first_piece = lax.rem(odd_y + apart, 2)
    piece = [lax.rem(first_piece + k, 2) for k in range(2)]
    if whole:
        hops = ((zn // 2, zn // 2 - 1), (zn // 2 - 1, zn // 2))
        held = list(range(zn))
    else:
        hops = ((REACH, REACH), (REACH, REACH))
        held = list(range(REACH + 1)) + list(range(zn - REACH, zn))

    def slab(behind):
        if behind <= 2:
            return near.at[behind]
        if behind >= zn - 2:
            return near.at[behind - (zn - 5)]
        if whole or behind <= REACH:
            return far.at[behind - 3]
        return far.at[behind - 3 - (zn - 2 * REACH - 1)]

    def behind_of(way, hop):
        return hop if way == 0 else (zn - hop) % zn

    def to_core(behind, k):
        block = slab(behind).at[2 * c + k]
        return remote(block, block, cs.at[behind, k], cr.at[behind, k], (z, other, y))

    def from_core(behind, k):
        block = slab(behind).at[2 * (1 - c) + k]
        return remote(block, block, cs.at[behind, k], cr.at[behind, k], (z, other, y))

    def along(way, hop, k):
        return remote(
            slab(behind_of(way, hop - 1)).at[2 * c + k], slab(behind_of(way, hop)).at[2 * c + k],
            zs.at[way, hop, k], zr.at[way, hop, k], ((up, down)[way], op, y),
        )

    def hand_on(hop, turn):
        k = piece[turn]
        for way in range(2):
            if hop <= hops[way][turn]:
                if hop > 0:
                    along(way, hop, k).wait_recv()
                if hop < hops[way][turn]:
                    along(way, hop + 1, k).start()
                if hop > 0 or way == 0:
                    to_core(behind_of(way, hop), k).start()

    for turn in range(2):
        k = piece[turn]
        pltpu.make_async_copy(elements.at[0, k], near.at[0, 2 * c + k], own_recv.at[k]).wait()
        hand_on(0, turn)

    if whole:
        work = [z]
    else:
        found, early, late = assign(zn, z, pairs)
        flag[0] = found
        work = [jnp.maximum(early, 0), jnp.maximum(late, 0)]
    take_perambs.wait()

    def send_perambs(n):
        ps[n][y] = pv[work[n]]
        for d in range(1, 4):
            remote(ps[n].at[y], ps[n].at[y], qs.at[n, d], qr.at[n, d], (z, op, lax.rem(y + d, 4))).start()

    send_perambs(0)
    lane = iota((32, 128), 1) < 64
    low = iota((64, 128), 1) < 64
    bd[...] = jnp.zeros_like(bd)

    def matrices(n):
        for d in range(1, 4):
            remote(
                ps[n].at[y], ps[n].at[lax.rem(y + 4 - d, 4)], qs.at[n, d], qr.at[n, d], (z, op, y)
            ).wait_recv()

        def flat(l, carry, g):
            rows = ps[n][g, l].astype(F32)
            for t in range(32):
                s8[t * 8:t * 8 + 4, :] = rows[:, t * 128:(t + 1) * 128]
            for b in range(4):
                q = s8[pl.ds(b, 32, stride=8), :]
                r = pltpu.roll(q, 64, 1)
                n64[pl.ds(b * 64, 32, stride=2), :] = jnp.where(lane, q, r)
                n64[pl.ds(b * 64 + 1, 32, stride=2), :] = jnp.where(lane, r, q)
                qn[g, b, l] = n64[b * 64:(b + 1) * 64, :].astype(BF16)
            return carry

        for g in range(4):
            lax.fori_loop(0, 3, functools.partial(flat, g=g), 0)

        def blocks(b, carry):
            g, bb = b // 4, lax.rem(b, 4)
            q0s[pl.ds(b * 32, 32), :] = qn[g, bb, 0, pl.ds(32 * c, 32), :]
            q2 = qn[g, bb, 2]
            none = jnp.zeros_like(q2)
            for k in range(4):
                half = jnp.where(low, q2, none) if k % 2 == 0 else jnp.where(low, none, q2)
                bd[b, k * 64:(k + 1) * 64, (k // 2) * 128:(k // 2 + 1) * 128] = half
            return carry

        lax.fori_loop(0, 16, blocks, 0)
        row, column = iota((128, 128), 0), iota((128, 128), 1)
        for g in range(4):
            for lo in range(2):
                acc = jnp.zeros((64, 128), F32)
                for bb in range(4):
                    spot = (row < 64) & (lax.rem(row, 2) == lo) & (column == bb * 32 + row // 2)
                    acc += dot(qn[g, bb, 1], jnp.where(spot, 1.0, 0.0).astype(BF16))
                q1r[lo * 64:(lo + 1) * 64, g * 128:(g + 1) * 128] = acc.astype(BF16)

    def seek(time):
        behind = lax.rem(z + zn - time, zn)
        is_near = (behind <= 2) | (behind >= zn - 2)
        near_at = jnp.where(is_near, jnp.where(behind <= 2, behind, behind - (zn - 5)), 0)
        if whole:
            far_at = jnp.where(is_near, 0, behind - 3)
        else:
            far_at = jnp.where(behind <= REACH, behind - 3, behind - 3 - (zn - 2 * REACH - 1))
            far_at = jnp.clip(jnp.where(is_near, 0, far_at), 0, 2 * REACH - 5)
        return is_near, near_at, far_at

    def chip_at(d):
        xx, yy = lax.rem(x + d // 4, 4), lax.rem(y + lax.rem(d, 4), 4)
        return xx * 4 + yy, (z, 2 * xx + c, yy)

    def post(data, landed, send, recv):
        def one(d, carry):
            u, device = chip_at(d)
            remote(data.at[u], landed.at[chip], send.at[d], recv.at[chip], device).start()
            return carry

        return one

    def collect(landed, send, recv):
        def one(d, carry):
            e = lax.rem(chip + d, 16)
            remote(landed.at[e], landed.at[e], send.at[d], recv.at[e], (z, op, y)).wait_recv()
            return carry

        lax.fori_loop(1, 16, one, 0)

    def send_sink(n):
        is_near, near_at, far_at = seek(pairs[1, work[n]])
        for k in range(2):
            def lift(t, carry, k=k):
                columns = pl.ds(pl.multiple_of(t * 128, 128), 128)
                tile = jnp.where(is_near, near[near_at, 2 * c + k, :, columns].astype(F32),
                                 far[far_at, 2 * c + k, :, columns].astype(F32))
                t2[pl.ds(pl.multiple_of((k * 32 + t) * 24, 8), 16), :] = tile
                return carry

            lax.fori_loop(0, 32, lift, 0, unroll=8)

        def cut(u, carry):
            sink[n][u] = t2[pl.ds(u, 64, stride=24), :].astype(BF16)
            return carry

        lax.fori_loop(0, 16, cut, 0, unroll=8)
        lax.fori_loop(1, 16, post(sink[n], rsink[n], bsend.at[n], br.at[n]), 0)
        rsink[n][chip] = sink[n][chip]

    def step_one(n, only_near):
        is_near, near_at, far_at = seek(pairs[0, work[n]])

        def body(t, carry):
            columns = pl.ds(pl.multiple_of(t * 256, 256), 256)
            tile = near[near_at, :, :, columns]
            if not only_near:
                tile = jnp.where(is_near, tile.astype(F32), far[far_at, :, :, columns].astype(F32)).astype(BF16)
            first = dot(q0s[:, :64], tile.reshape(64, 256)).astype(BF16)
            v[:, t] = first.reshape(16, 32, 256)
            return carry

        lax.fori_loop(0, 16, body, 0, unroll=8)

    def step_two():
        def body(b, carry):
            second = dot(v[b].reshape(512, 256), bd[b], NT)
            for n in range(16):
                for h in range(2):
                    start = pl.multiple_of((b * 32 + n * 2 + h) * PITCH, 8)
                    t2[pl.ds(start, 32), :] = second[n * 32:(n + 1) * 32, h * 128:(h + 1) * 128]
            return carry

        lax.fori_loop(0, 16, body, 0, unroll=8)

    def step_three(n):
        def body(d, carry):
            u = chip_at(lax.rem(d, 16))[0]
            left = t2[pl.ds(u, 512, stride=PITCH), :].astype(BF16)
            right = t2[pl.ds(u + 16, 512, stride=PITCH), :].astype(BF16)
            both = dot(q1r[...], jnp.concatenate([left, right], axis=1))
            even = both[:64, :128] + pltpu.roll(both[64:, :128], 64, 1)
            odd = pltpu.roll(both[:64, 128:], 64, 1) + both[64:, 128:]
            prod[n][u] = jnp.where(low, even, odd).astype(BF16)
            return carry

        for start in (1, 5, 9, 13):
            lax.fori_loop(start, start + 4, body, 0, unroll=4)
            send = post(prod[n], rprod[n], asend.at[n], ar.at[n])
            lax.fori_loop(start, min(start + 4, 16), send, 0)
        rprod[n][chip] = prod[n][chip]

    if whole:
        for hop in range(1, max(hops[0]) + 1):
            for turn in range(2):
                hand_on(hop, turn)
            if hop == 1:
                matrices(0)
        for behind in held:
            for k in range(2):
                from_core(behind, k).wait_recv()
    else:
        for turn in range(2):
            hand_on(1, turn)
        matrices(0)
        for turn in range(2):
            hand_on(2, turn)
        send_perambs(1)
        close = [b for b in held if b <= 2 or b >= zn - 2]
        for behind in close:
            for k in range(2):
                from_core(behind, k).wait_recv()
        step_one(0, True)
        hand_on(3, 0)
        step_two()
        hand_on(3, 1)
        step_three(0)
        hand_on(4, 0)
        matrices(1)
        hand_on(4, 1)
        for away in (REACH, zn - REACH):
            pl.semaphore_signal(
                token, inc=1, device_id=(lax.rem(z + away, zn), op, y), device_id_type=MESH
            )
        for behind in held:
            if behind not in close:
                for k in range(2):
                    from_core(behind, k).wait_recv()

    last = slots - 1
    for n in reversed(range(slots)):
        send_sink(n)
    step_one(last, False)
    step_two()
    step_three(last)

    lane16 = iota((16, 128), 1) < 64
    wl, wj = iota((16, 128), 0), iota((16, 128), 1)

    def contract(n):
        collect(rsink[n], bsend.at[n], br.at[n])
        for i in range(16):
            t2[i * 72:i * 72 + 64, :] = rsink[n][i].astype(F32)
        for r in range(64):
            ks[:, r * 128:(r + 1) * 128] = t2[pl.ds(r, 16, stride=72), :].astype(BF16)
        collect(rprod[n], asend.at[n], ar.at[n])
        for j in range(16):
            t2[j * 72:j * 72 + 64, :] = rprod[n][j].astype(F32)
        for t in range(32):
            a = t2[pl.ds(2 * t, 16, stride=72), :]
            b = t2[pl.ds(2 * t + 1, 16, stride=72), :]
            kp[:, t * 128:(t + 1) * 128] = jnp.where(lane16, a, pltpu.roll(b, 64, 1)).astype(BF16)
            kp[:, (32 + t) * 128:(33 + t) * 128] = jnp.where(lane16, pltpu.roll(a, 64, 1), b).astype(BF16)
        square = dot(ks[...], kp[...], NT)
        table = dot(square, jnp.where(wl == lax.rem(wj, 16), 1.0, 0.0).astype(F32), precision=lax.Precision.HIGHEST)
        mine = jnp.where(wj // 16 == lax.rem(wl, 8), table, 0.0)
        return jnp.sum(mine.reshape(2, 8, 128), axis=1)

    tables = [contract(n) for n in range(slots)]
    place = op * 4 + y
    if whole:
        part[place] = tables[0]
    else:
        pl.semaphore_wait(token, 2)
        for d in range(zn):
            p = lax.rem(z + d, zn)
            zout[d] = jnp.where(early == p, tables[0], 0.0) + jnp.where(late == p, tables[1], 0.0)
            if d > 0:
                remote(zout.at[d], zin.at[d], ws.at[d], wr.at[d], (p, op, y)).start()
        zin[0] = zout[0]
        for d in range(1, zn):
            remote(zout.at[d], zin.at[d], ws.at[d], wr.at[d], (z, op, y)).wait_recv()
        part[place] = jnp.sum(zin[...], axis=0)

    def tell(d):
        o, s = lax.rem(op + d // 4, 8), lax.rem(y + d % 4, 4)
        return remote(part.at[place], part.at[place], rs.at[d], rr.at[d], (z, o, s))

    def told(d):
        o, s = lax.rem(op + 8 - d // 4, 8), lax.rem(y + 4 - d % 4, 4)
        return remote(part.at[place], part.at[o * 4 + s], rs.at[d], rr.at[d], (z, op, y))

    for d in range(1, 32):
        tell(d).start()
    for d in range(1, 32):
        told(d).wait_recv()
    out[...] = jnp.sum(part[...], axis=0)

    for k in range(2):
        @pl.when(2 * c + k != y)
        def _(k=k):
            remote(elements.at[0, k], near.at[0, y], own_send.at[k], own_recv.at[k], (z, op, y)).wait_send()

        for way in range(2):
            for hop in range(1, hops[way][k] + 1):
                along(way, hop, piece[k]).wait_send()
        for behind in held:
            to_core(behind, k).wait_send()
    for n in range(slots):
        for d in range(1, 4):
            remote(ps[n].at[y], ps[n].at[y], qs.at[n, d], qr.at[n, d], (z, op, y)).wait_send()

        def left(d, carry, n=n):
            remote(sink[n].at[0], rsink[n].at[0], bsend.at[n, d], br.at[n, 0], (z, op, y)).wait_send()
            remote(prod[n].at[0], rprod[n].at[0], asend.at[n, d], ar.at[n, 0], (z, op, y)).wait_send()
            return carry

        lax.fori_loop(1, 16, left, 0)

    for d in range(1, 32):
        tell(d).wait_send()
    if not whole:
        for d in range(1, zn):
            remote(zout.at[d], zin.at[d], ws.at[d], wr.at[d], (z, op, y)).wait_send()


def call(zn, whole, pairs, elements, perambs):
    dma = pltpu.SemaphoreType.DMA
    slots = 1 if whole else 2
    far = zn - 5 if whole else 2 * REACH - 4
    out_shape = [jax.ShapeDtypeStruct((2, 128), F32)]
    out_specs = [pl.BlockSpec(memory_space=pltpu.VMEM)]
    if not whole:
        out_shape.append(jax.ShapeDtypeStruct((1,), jnp.int32))
        out_specs.append(pl.BlockSpec(memory_space=pltpu.SMEM))
    return pl.pallas_call(
        functools.partial(kernel, zn, whole),
        out_shape=out_shape,
        in_specs=[
            pl.BlockSpec(memory_space=pltpu.SMEM),
            pl.BlockSpec(memory_space=pl.ANY),
            pl.BlockSpec(memory_space=pl.ANY),
        ],
        out_specs=out_specs,
        scratch_shapes=[
            *[pltpu.VMEM((4, 3, 4, 4096), BF16)] * slots,
            *[pltpu.VMEM((16, 64, 128), BF16)] * (4 * slots),
            pltpu.VMEM((5, 4, 16, 4096), BF16),
            pltpu.VMEM((far, 4, 16, 4096), BF16),
            pltpu.VMEM((16, 3, 4, 4096), BF16),
            pltpu.VMEM((256, 128), F32),
            pltpu.VMEM((256, 128), F32),
            pltpu.VMEM((4, 4, 3, 64, 128), BF16),
            pltpu.VMEM((512, 128), BF16),
            pltpu.VMEM((16, 256, 256), BF16),
            pltpu.VMEM((128, 512), BF16),
            pltpu.VMEM((16, 16, 32, 256), BF16),
            pltpu.VMEM((512 * PITCH, 128), F32),
            pltpu.VMEM((16, 8192), BF16),
            pltpu.VMEM((16, 8192), BF16),
            pltpu.VMEM((32, 2, 128), F32),
            pltpu.VMEM((zn, 2, 128), F32),
            pltpu.VMEM((zn, 2, 128), F32),
            dma, dma((2,)), dma((2,)),
            dma((2, zn, 2)), dma((2, zn, 2)), dma((zn, 2)), dma((zn, 2)),
            dma((slots, 4)), dma((slots, 4)),
            dma((slots, 16)), dma((slots, 16)), dma((slots, 16)), dma((slots, 16)), dma((32,)), dma((32,)),
            dma((zn,)), dma((zn,)), pltpu.SemaphoreType.REGULAR,
        ],
        compiler_params=pltpu.CompilerParams(
            collective_id=1 if whole else 0, has_side_effects=True, vmem_limit_bytes=56 * 1024 * 1024
        ),
    )(pairs, elements, perambs)


def solution(mesh):
    zn = mesh.shape["tm"]

    def body(pairs, elements, perambs):
        given = (pairs.T, elements, perambs.transpose(0, 2, 1, 3))
        table, found = call(zn, False, *given)
        table = lax.cond(found[0] == 1, lambda: table, lambda: call(zn, True, *given)[0])
        return table.reshape(1, 16, 16)

    placed = (P(), P("tm", "op", "spin", None), P(None, "spin", None, None))
    return jax.shard_map(
        body, mesh=mesh, in_specs=placed, out_specs=P("tm", None, None), check_vma=False
    )
```

```python
import functools

import jax
import jax.numpy as jnp
from jax import lax
from jax.experimental import pallas as pl
from jax.experimental.pallas import tpu as pltpu
from jax.sharding import PartitionSpec as P

MESH = pl.DeviceIdType.MESH
F32 = jnp.float32
BF16 = jnp.bfloat16
NN = (((1,), (0,)), ((), ()))
NT = (((1,), (1,)), ((), ()))
PITCH = 40
REACH = 4
FAR_CHIPS = sorted(range(1, 16), key=lambda d: -(min(d // 4, 4 - d // 4) + min(d % 4, 4 - d % 4)))
FAR_PLACES = sorted(range(1, 32), key=lambda d: -(min(d // 4, 8 - d // 4) / 2 + min(d % 4, 4 - d % 4)))
TRIES = ((1, 0), (-1, 0), (1, 8), (-1, 8))


def dot(a, b, dims=NN, precision=None):
    return lax.dot_general(a, b, dims, precision=precision, preferred_element_type=F32)


def iota(shape, axis):
    return lax.broadcasted_iota(jnp.int32, shape, axis)


def assign(zn, z, pairs):
    full = (1 << zn) - 1

    def window(centre, reach):
        mask = lax.shift_left(jnp.int32((1 << (2 * reach + 1)) - 1), lax.rem(centre + zn - reach, zn))
        return (mask | lax.shift_right_logical(mask, jnp.int32(zn))) & full

    found, early, late = jnp.int32(0), jnp.int32(-1), jnp.int32(-1)
    for sign, turn in TRIES:
        own = lax.shift_left(jnp.int32(1), lax.rem(sign * z + turn + zn, zn))

        def place(p, state, sign=sign, turn=turn, own=own):
            free_early, free_late, good, mine_early, mine_late = state
            source = lax.rem(sign * pairs[0, p] + turn + zn, zn)
            sink = lax.rem(sign * pairs[1, p] + turn + zn, zn)
            around = window(sink, REACH)
            near = window(source, 2) & around & free_early
            wide = window(source, REACH) & around & free_late
            at_early = near & -near
            at_late = jnp.where(near == 0, wide & -wide, 0)
            return (
                free_early - at_early,
                free_late - at_late,
                jnp.where((at_early | at_late) == 0, 0, good),
                jnp.where(at_early == own, p, mine_early),
                jnp.where(at_late == own, p, mine_late),
            )

        start = (jnp.int32(full), jnp.int32(full), jnp.int32(1), jnp.int32(-1), jnp.int32(-1))
        _, _, good, mine_early, mine_late = lax.fori_loop(0, zn, place, start, unroll=4)
        early = jnp.where(found == 1, early, mine_early)
        late = jnp.where(found == 1, late, mine_late)
        found = jnp.maximum(found, good)
    return found, early, late


def kernel(zn, whole, pairs, elements, perambs, out, *rest):
    if whole:
        flag, rest = None, rest
    else:
        flag, rest = rest[0], rest[1:]
    slots = 1 if whole else 2
    own, rest = rest[:5 * slots], rest[5 * slots:]
    ps, prod, sink, rprod, rsink = (own[i * slots:(i + 1) * slots] for i in range(5))
    (near, far, pv, s8, n64, qn, q0s, bd, q1r, v, t2, ks, kp, part, zout, zin,
     pv_sem, own_recv, own_send, zr, zs, cr, cs, qr, qs, ar, asend, br, bsend, rr, rs, wr, ws, token) = rest
    z, op, y = lax.axis_index("tm"), lax.axis_index("op"), lax.axis_index("spin")
    x, c = op // 2, lax.rem(op, 2)
    chip = x * 4 + y
    other = op + 1 - 2 * c
    up, down = lax.rem(z + 1, zn), lax.rem(z + zn - 1, zn)

    def remote(src, dst, send, recv, device):
        return pltpu.make_async_remote_copy(
            src_ref=src, dst_ref=dst, send_sem=send, recv_sem=recv, device_id=device, device_id_type=MESH
        )

    take_perambs = pltpu.make_async_copy(perambs, pv, pv_sem)
    take_perambs.start()

    barrier = pltpu.get_barrier_semaphore()

    def greet(i, carry):
        o, s = i // 4, lax.rem(i, 4)

        @pl.when(i != op * 4 + y)
        def _():
            pl.semaphore_signal(barrier, inc=1, device_id=(z, o, s), device_id_type=MESH)

        return carry

    lax.fori_loop(0, 32, greet, 0)
    for place in (up, down):
        pl.semaphore_signal(barrier, inc=1, device_id=(place, op, y), device_id_type=MESH)
    pl.semaphore_wait(barrier, 33)

    odd_y = lax.rem(y, 2)
    for k in range(2):
        j = lax.rem(k + 1 - odd_y, 2)
        target = 2 * c + j

        @pl.when(target != y)
        def _(j=j, target=target):
            remote(
                elements.at[0, j], near.at[0, y], own_send.at[j], own_recv.at[odd_y], (z, 2 * x + y // 2, target)
            ).start()

        @pl.when(target == y)
        def _(j=j):
            pltpu.make_async_copy(elements.at[0, j], near.at[0, y], own_recv.at[odd_y]).start()

    apart = lax.rem(c + y // 2, 2)
    first_piece = lax.rem(odd_y + apart, 2)
    piece = [lax.rem(first_piece + k, 2) for k in range(2)]
    if whole:
        hops = ((zn // 2, zn // 2 - 1), (zn // 2 - 1, zn // 2))
        held = list(range(zn))
    else:
        hops = ((REACH, REACH), (REACH, REACH))
        held = list(range(REACH + 1)) + list(range(zn - REACH, zn))

    def slab(behind):
        if behind <= 2:
            return near.at[behind]
        if behind >= zn - 2:
            return near.at[behind - (zn - 5)]
        if whole or behind <= REACH:
            return far.at[behind - 3]
        return far.at[behind - 3 - (zn - 2 * REACH - 1)]

    def behind_of(way, hop):
        return hop if way == 0 else (zn - hop) % zn

    def to_core(behind, k):
        block = slab(behind).at[2 * c + k]
        return remote(block, block, cs.at[behind, k], cr.at[behind, k], (z, other, y))

    def from_core(behind, k):
        block = slab(behind).at[2 * (1 - c) + k]
        return remote(block, block, cs.at[behind, k], cr.at[behind, k], (z, other, y))

    def along(way, hop, k):
        return remote(
            slab(behind_of(way, hop - 1)).at[2 * c + k], slab(behind_of(way, hop)).at[2 * c + k],
            zs.at[way, hop, k], zr.at[way, hop, k], ((up, down)[way], op, y),
        )

    def hand_on(hop, turn):
        k = piece[turn]
        for way in range(2):
            if hop <= hops[way][turn]:
                if hop > 0:
                    along(way, hop, k).wait_recv()
                if hop < hops[way][turn]:
                    along(way, hop + 1, k).start()
                if hop > 0 or way == 0:
                    to_core(behind_of(way, hop), k).start()

    for turn in range(2):
        k = piece[turn]
        pltpu.make_async_copy(elements.at[0, k], near.at[0, 2 * c + k], own_recv.at[k]).wait()
        hand_on(0, turn)

    if whole:
        work = [z]
    else:
        found, early, late = assign(zn, z, pairs)
        flag[0] = found
        work = [jnp.maximum(early, 0), jnp.maximum(late, 0)]
    take_perambs.wait()

    def send_perambs(n):
        ps[n][y] = pv[work[n]]
        for d in range(1, 4):
            remote(ps[n].at[y], ps[n].at[y], qs.at[n, d], qr.at[n, d], (z, op, lax.rem(y + d, 4))).start()

    send_perambs(0)
    lane = iota((32, 128), 1) < 64
    low = iota((64, 128), 1) < 64
    bd[...] = jnp.zeros_like(bd)

    def matrices(n):
        for d in range(1, 4):
            remote(
                ps[n].at[y], ps[n].at[lax.rem(y + 4 - d, 4)], qs.at[n, d], qr.at[n, d], (z, op, y)
            ).wait_recv()

        def flat(l, carry, g):
            rows = ps[n][g, l].astype(F32)
            for t in range(32):
                s8[t * 8:t * 8 + 4, :] = rows[:, t * 128:(t + 1) * 128]
            for b in range(4):
                q = s8[pl.ds(b, 32, stride=8), :]
                r = pltpu.roll(q, 64, 1)
                n64[pl.ds(b * 64, 32, stride=2), :] = jnp.where(lane, q, r)
                n64[pl.ds(b * 64 + 1, 32, stride=2), :] = jnp.where(lane, r, q)
                qn[g, b, l] = n64[b * 64:(b + 1) * 64, :].astype(BF16)
            return carry

        for g in range(4):
            lax.fori_loop(0, 3, functools.partial(flat, g=g), 0)

        def blocks(b, carry):
            g, bb = b // 4, lax.rem(b, 4)
            q0s[pl.ds(b * 32, 32), :] = qn[g, bb, 0, pl.ds(32 * c, 32), :]
            q2 = qn[g, bb, 2]
            none = jnp.zeros_like(q2)
            for k in range(4):
                half = jnp.where(low, q2, none) if k % 2 == 0 else jnp.where(low, none, q2)
                bd[b, k * 64:(k + 1) * 64, (k // 2) * 128:(k // 2 + 1) * 128] = half
            return carry

        lax.fori_loop(0, 16, blocks, 0)
        row, column = iota((128, 128), 0), iota((128, 128), 1)
        for g in range(4):
            for lo in range(2):
                acc = jnp.zeros((64, 128), F32)
                for bb in range(4):
                    spot = (row < 64) & (lax.rem(row, 2) == lo) & (column == bb * 32 + row // 2)
                    acc += dot(qn[g, bb, 1], jnp.where(spot, 1.0, 0.0).astype(BF16))
                q1r[lo * 64:(lo + 1) * 64, g * 128:(g + 1) * 128] = acc.astype(BF16)

    def seek(time):
        behind = lax.rem(z + zn - time, zn)
        is_near = (behind <= 2) | (behind >= zn - 2)
        near_at = jnp.where(is_near, jnp.where(behind <= 2, behind, behind - (zn - 5)), 0)
        if whole:
            far_at = jnp.where(is_near, 0, behind - 3)
        else:
            far_at = jnp.where(behind <= REACH, behind - 3, behind - 3 - (zn - 2 * REACH - 1))
            far_at = jnp.clip(jnp.where(is_near, 0, far_at), 0, 2 * REACH - 5)
        return is_near, near_at, far_at

    def chip_at(d):
        xx, yy = lax.rem(x + d // 4, 4), lax.rem(y + d % 4, 4)
        return xx * 4 + yy, (z, 2 * xx + c, yy)

    def post(data, landed, send, recv):
        def one(d, carry):
            u, device = chip_at(d)
            remote(data.at[u], landed.at[chip], send.at[d], recv.at[chip], device).start()
            return carry

        return one

    def collect(landed, send, recv):
        def one(d, carry):
            e = lax.rem(chip + d, 16)
            remote(landed.at[e], landed.at[e], send.at[d], recv.at[e], (z, op, y)).wait_recv()
            return carry

        lax.fori_loop(1, 16, one, 0)

    def send_sink(n):
        is_near, near_at, far_at = seek(pairs[1, work[n]])
        for k in range(2):
            def lift(t, carry, k=k):
                columns = pl.ds(pl.multiple_of(t * 128, 128), 128)
                tile = jnp.where(is_near, near[near_at, 2 * c + k, :, columns].astype(F32),
                                 far[far_at, 2 * c + k, :, columns].astype(F32))
                t2[pl.ds(pl.multiple_of((k * 32 + t) * 24, 8), 16), :] = tile
                return carry

            lax.fori_loop(0, 32, lift, 0, unroll=8)

        def cut(u, carry):
            sink[n][u] = t2[pl.ds(u, 64, stride=24), :].astype(BF16)
            return carry

        lax.fori_loop(0, 16, cut, 0, unroll=8)
        send = post(sink[n], rsink[n], bsend.at[n], br.at[n])
        for d in FAR_CHIPS:
            send(d, 0)
        rsink[n][chip] = sink[n][chip]

    def step_one(n, only_near):
        is_near, near_at, far_at = seek(pairs[0, work[n]])

        def body(t, carry):
            columns = pl.ds(pl.multiple_of(t * 256, 256), 256)
            tile = near[near_at, :, :, columns]
            if not only_near:
                tile = jnp.where(is_near, tile.astype(F32), far[far_at, :, :, columns].astype(F32)).astype(BF16)
            first = dot(q0s[:, :64], tile.reshape(64, 256)).astype(BF16)
            v[:, t] = first.reshape(16, 32, 256)
            return carry

        lax.fori_loop(0, 16, body, 0, unroll=16)

    def step_two():
        def body(b, carry):
            second = dot(v[b].reshape(512, 256), bd[b], NT)
            for n in range(16):
                for h in range(2):
                    start = pl.multiple_of((b * 32 + n * 2 + h) * PITCH, 8)
                    t2[pl.ds(start, 32), :] = second[n * 32:(n + 1) * 32, h * 128:(h + 1) * 128]
            return carry

        lax.fori_loop(0, 16, body, 0, unroll=16)

    def step_three(n):
        def body(d, carry):
            u = chip_at(d)[0]
            left = t2[pl.ds(u, 512, stride=PITCH), :].astype(BF16)
            right = t2[pl.ds(u + 16, 512, stride=PITCH), :].astype(BF16)
            both = dot(q1r[...], jnp.concatenate([left, right], axis=1))
            even = both[:64, :128] + pltpu.roll(both[64:, :128], 64, 1)
            odd = pltpu.roll(both[:64, 128:], 64, 1) + both[64:, 128:]
            prod[n][u] = jnp.where(low, even, odd).astype(BF16)
            return carry

        order = FAR_CHIPS + [0]
        send = post(prod[n], rprod[n], asend.at[n], ar.at[n])
        for start in (0, 4, 8, 12):
            for d in order[start:start + 4]:
                body(d, 0)
            for d in order[start:start + 4]:
                if d:
                    send(d, 0)
        rprod[n][chip] = prod[n][chip]

    if whole:
        for hop in range(1, max(hops[0]) + 1):
            for turn in range(2):
                hand_on(hop, turn)
            if hop == 1:
                matrices(0)
        for behind in held:
            for k in range(2):
                from_core(behind, k).wait_recv()
    else:
        for turn in range(2):
            hand_on(1, turn)
        matrices(0)
        for turn in range(2):
            hand_on(2, turn)
        send_perambs(1)
        close = [b for b in held if b <= 2 or b >= zn - 2]
        for behind in close:
            for k in range(2):
                from_core(behind, k).wait_recv()
        step_one(0, True)
        hand_on(3, 0)
        step_two()
        hand_on(3, 1)
        step_three(0)
        hand_on(4, 0)
        matrices(1)
        hand_on(4, 1)
        for away in (REACH, zn - REACH):
            pl.semaphore_signal(
                token, inc=1, device_id=(lax.rem(z + away, zn), op, y), device_id_type=MESH
            )
        for behind in held:
            if behind not in close:
                for k in range(2):
                    from_core(behind, k).wait_recv()

    last = slots - 1
    for n in reversed(range(slots)):
        send_sink(n)
    step_one(last, False)
    step_two()
    step_three(last)

    lane16 = iota((16, 128), 1) < 64
    wl, wj = iota((16, 128), 0), iota((16, 128), 1)

    def contract(n):
        collect(rsink[n], bsend.at[n], br.at[n])
        for i in range(16):
            t2[i * 72:i * 72 + 64, :] = rsink[n][i].astype(F32)
        for r in range(64):
            ks[:, r * 128:(r + 1) * 128] = t2[pl.ds(r, 16, stride=72), :].astype(BF16)
        collect(rprod[n], asend.at[n], ar.at[n])
        for j in range(16):
            t2[j * 72:j * 72 + 64, :] = rprod[n][j].astype(F32)
        for t in range(32):
            a = t2[pl.ds(2 * t, 16, stride=72), :]
            b = t2[pl.ds(2 * t + 1, 16, stride=72), :]
            kp[:, t * 128:(t + 1) * 128] = jnp.where(lane16, a, pltpu.roll(b, 64, 1)).astype(BF16)
            kp[:, (32 + t) * 128:(33 + t) * 128] = jnp.where(lane16, pltpu.roll(a, 64, 1), b).astype(BF16)
        square = dot(ks[...], kp[...], NT)
        table = dot(square, jnp.where(wl == lax.rem(wj, 16), 1.0, 0.0).astype(F32), precision=lax.Precision.HIGHEST)
        mine = jnp.where(wj // 16 == lax.rem(wl, 8), table, 0.0)
        return jnp.sum(mine.reshape(2, 8, 128), axis=1)

    tables = [contract(n) for n in range(slots)]
    place = op * 4 + y
    if whole:
        part[place] = tables[0]
    else:
        pl.semaphore_wait(token, 2)
        for d in sorted(range(zn), key=lambda d: -min(d, zn - d)):
            p = lax.rem(z + d, zn)
            zout[d] = jnp.where(early == p, tables[0], 0.0) + jnp.where(late == p, tables[1], 0.0)
            if d > 0:
                remote(zout.at[d], zin.at[d], ws.at[d], wr.at[d], (p, op, y)).start()
        zin[0] = zout[0]
        for d in range(1, zn):
            remote(zout.at[d], zin.at[d], ws.at[d], wr.at[d], (z, op, y)).wait_recv()
        part[place] = jnp.sum(zin[...], axis=0)

    def tell(d):
        o, s = lax.rem(op + d // 4, 8), lax.rem(y + d % 4, 4)
        return remote(part.at[place], part.at[place], rs.at[d], rr.at[d], (z, o, s))

    def told(d):
        o, s = lax.rem(op + 8 - d // 4, 8), lax.rem(y + 4 - d % 4, 4)
        return remote(part.at[place], part.at[o * 4 + s], rs.at[d], rr.at[d], (z, op, y))

    for d in FAR_PLACES:
        tell(d).start()
    for d in range(1, 32):
        told(d).wait_recv()
    out[...] = jnp.sum(part[...], axis=0)

    for k in range(2):
        @pl.when(2 * c + k != y)
        def _(k=k):
            remote(elements.at[0, k], near.at[0, y], own_send.at[k], own_recv.at[k], (z, op, y)).wait_send()

        for way in range(2):
            for hop in range(1, hops[way][k] + 1):
                along(way, hop, piece[k]).wait_send()
        for behind in held:
            to_core(behind, k).wait_send()
    for n in range(slots):
        for d in range(1, 4):
            remote(ps[n].at[y], ps[n].at[y], qs.at[n, d], qr.at[n, d], (z, op, y)).wait_send()

        def left(d, carry, n=n):
            remote(sink[n].at[0], rsink[n].at[0], bsend.at[n, d], br.at[n, 0], (z, op, y)).wait_send()
            remote(prod[n].at[0], rprod[n].at[0], asend.at[n, d], ar.at[n, 0], (z, op, y)).wait_send()
            return carry

        lax.fori_loop(1, 16, left, 0)

    for d in range(1, 32):
        tell(d).wait_send()
    if not whole:
        for d in range(1, zn):
            remote(zout.at[d], zin.at[d], ws.at[d], wr.at[d], (z, op, y)).wait_send()


def call(zn, whole, pairs, elements, perambs):
    dma = pltpu.SemaphoreType.DMA
    slots = 1 if whole else 2
    far = zn - 5 if whole else 2 * REACH - 4
    out_shape = [jax.ShapeDtypeStruct((2, 128), F32)]
    out_specs = [pl.BlockSpec(memory_space=pltpu.VMEM)]
    if not whole:
        out_shape.append(jax.ShapeDtypeStruct((1,), jnp.int32))
        out_specs.append(pl.BlockSpec(memory_space=pltpu.SMEM))
    return pl.pallas_call(
        functools.partial(kernel, zn, whole),
        out_shape=out_shape,
        in_specs=[
            pl.BlockSpec(memory_space=pltpu.SMEM),
            pl.BlockSpec(memory_space=pl.ANY),
            pl.BlockSpec(memory_space=pl.ANY),
        ],
        out_specs=out_specs,
        scratch_shapes=[
            *[pltpu.VMEM((4, 3, 4, 4096), BF16)] * slots,
            *[pltpu.VMEM((16, 64, 128), BF16)] * (4 * slots),
            pltpu.VMEM((5, 4, 16, 4096), BF16),
            pltpu.VMEM((far, 4, 16, 4096), BF16),
            pltpu.VMEM((16, 3, 4, 4096), BF16),
            pltpu.VMEM((256, 128), F32),
            pltpu.VMEM((256, 128), F32),
            pltpu.VMEM((4, 4, 3, 64, 128), BF16),
            pltpu.VMEM((512, 128), BF16),
            pltpu.VMEM((16, 256, 256), BF16),
            pltpu.VMEM((128, 512), BF16),
            pltpu.VMEM((16, 16, 32, 256), BF16),
            pltpu.VMEM((512 * PITCH, 128), F32),
            pltpu.VMEM((16, 8192), BF16),
            pltpu.VMEM((16, 8192), BF16),
            pltpu.VMEM((32, 2, 128), F32),
            pltpu.VMEM((zn, 2, 128), F32),
            pltpu.VMEM((zn, 2, 128), F32),
            dma, dma((2,)), dma((2,)),
            dma((2, zn, 2)), dma((2, zn, 2)), dma((zn, 2)), dma((zn, 2)),
            dma((slots, 4)), dma((slots, 4)),
            dma((slots, 16)), dma((slots, 16)), dma((slots, 16)), dma((slots, 16)), dma((32,)), dma((32,)),
            dma((zn,)), dma((zn,)), pltpu.SemaphoreType.REGULAR,
        ],
        compiler_params=pltpu.CompilerParams(
            collective_id=1 if whole else 0, has_side_effects=True, vmem_limit_bytes=56 * 1024 * 1024
        ),
    )(pairs, elements, perambs)


def solution(mesh):
    zn = mesh.shape["tm"]

    def body(pairs, elements, perambs):
        given = (pairs.T, elements, perambs.transpose(0, 2, 1, 3))
        table, found = call(zn, False, *given)
        table = lax.cond(found[0] == 1, lambda: table, lambda: call(zn, True, *given)[0])
        return table.reshape(1, 16, 16)

    placed = (P(), P("tm", "op", "spin", None), P(None, "spin", None, None))
    return jax.shard_map(
        body, mesh=mesh, in_specs=placed, out_specs=P("tm", None, None), check_vma=False
    )
```

```python
import functools

import jax
import jax.numpy as jnp
from jax import lax
from jax.experimental import pallas as pl
from jax.experimental.pallas import tpu as pltpu
from jax.sharding import PartitionSpec as P

MESH = pl.DeviceIdType.MESH
F32 = jnp.float32
BF16 = jnp.bfloat16
NN = (((1,), (0,)), ((), ()))
NT = (((1,), (1,)), ((), ()))
PITCH = 40
REACH = 4
FAR_CHIPS = sorted(range(1, 16), key=lambda d: -(min(d // 4, 4 - d // 4) + min(d % 4, 4 - d % 4)))
FAR_PLACES = sorted(range(1, 32), key=lambda d: -(min(d // 4, 8 - d // 4) / 2 + min(d % 4, 4 - d % 4)))
TRIES = ((1, 0), (-1, 0), (1, 8), (-1, 8))


def dot(a, b, dims=NN, precision=None):
    return lax.dot_general(a, b, dims, precision=precision, preferred_element_type=F32)


def iota(shape, axis):
    return lax.broadcasted_iota(jnp.int32, shape, axis)


def assign(zn, z, pairs):
    full = (1 << zn) - 1

    def window(centre, reach):
        mask = lax.shift_left(jnp.int32((1 << (2 * reach + 1)) - 1), lax.rem(centre + zn - reach, zn))
        return (mask | lax.shift_right_logical(mask, jnp.int32(zn))) & full

    found, early, late = jnp.int32(0), jnp.int32(-1), jnp.int32(-1)
    for sign, turn in TRIES:
        own = lax.shift_left(jnp.int32(1), lax.rem(sign * z + turn + zn, zn))

        def place(p, state, sign=sign, turn=turn, own=own):
            free_early, free_late, good, mine_early, mine_late = state
            source = lax.rem(sign * pairs[0, p] + turn + zn, zn)
            sink = lax.rem(sign * pairs[1, p] + turn + zn, zn)
            around = window(sink, REACH)
            near = window(source, 2) & around & free_early
            wide = window(source, REACH) & around & free_late
            at_early = near & -near
            at_late = jnp.where(near == 0, wide & -wide, 0)
            return (
                free_early - at_early,
                free_late - at_late,
                jnp.where((at_early | at_late) == 0, 0, good),
                jnp.where(at_early == own, p, mine_early),
                jnp.where(at_late == own, p, mine_late),
            )

        start = (jnp.int32(full), jnp.int32(full), jnp.int32(1), jnp.int32(-1), jnp.int32(-1))
        _, _, good, mine_early, mine_late = lax.fori_loop(0, zn, place, start, unroll=4)
        early = jnp.where(found == 1, early, mine_early)
        late = jnp.where(found == 1, late, mine_late)
        found = jnp.maximum(found, good)
    return found, early, late


def kernel(zn, whole, pairs, elements, perambs, out, *rest):
    if whole:
        flag, rest = None, rest
    else:
        flag, rest = rest[0], rest[1:]
    slots = 1 if whole else 2
    own, rest = rest[:5 * slots], rest[5 * slots:]
    ps, prod, sink, rprod, rsink = (own[i * slots:(i + 1) * slots] for i in range(5))
    (near, far, pv, s8, n64, qn, q0s, bd, q1r, v, t2, ks, kp, part, zout, zin,
     pv_sem, own_recv, own_send, zr, zs, cr, cs, qr, qs, ar, asend, br, bsend, rr, rs, wr, ws, token) = rest
    z, op, y = lax.axis_index("tm"), lax.axis_index("op"), lax.axis_index("spin")
    x, c = op // 2, lax.rem(op, 2)
    chip = x * 4 + y
    other = op + 1 - 2 * c
    up, down = lax.rem(z + 1, zn), lax.rem(z + zn - 1, zn)

    def remote(src, dst, send, recv, device):
        return pltpu.make_async_remote_copy(
            src_ref=src, dst_ref=dst, send_sem=send, recv_sem=recv, device_id=device, device_id_type=MESH
        )

    take_perambs = pltpu.make_async_copy(perambs, pv, pv_sem)
    take_perambs.start()

    barrier = pltpu.get_barrier_semaphore()

    def greet(i, carry):
        o, s = i // 4, lax.rem(i, 4)

        @pl.when(i != op * 4 + y)
        def _():
            pl.semaphore_signal(barrier, inc=1, device_id=(z, o, s), device_id_type=MESH)

        return carry

    lax.fori_loop(0, 32, greet, 0)
    for place in (up, down):
        pl.semaphore_signal(barrier, inc=1, device_id=(place, op, y), device_id_type=MESH)
    pl.semaphore_wait(barrier, 33)

    odd_y = lax.rem(y, 2)
    for k in range(2):
        j = lax.rem(k + 1 - odd_y, 2)
        target = 2 * c + j

        @pl.when(target != y)
        def _(j=j, target=target):
            remote(
                elements.at[0, j], near.at[0, y], own_send.at[j], own_recv.at[odd_y], (z, 2 * x + y // 2, target)
            ).start()

        @pl.when(target == y)
        def _(j=j):
            pltpu.make_async_copy(elements.at[0, j], near.at[0, y], own_recv.at[odd_y]).start()

    apart = lax.rem(c + y // 2, 2)
    first_piece = lax.rem(odd_y + apart, 2)
    piece = [lax.rem(first_piece + k, 2) for k in range(2)]
    if whole:
        hops = ((zn // 2, zn // 2 - 1), (zn // 2 - 1, zn // 2))
        held = list(range(zn))
    else:
        hops = ((REACH, REACH), (REACH, REACH))
        held = list(range(REACH + 1)) + list(range(zn - REACH, zn))

    def slab(behind):
        if behind <= 2:
            return near.at[behind]
        if behind >= zn - 2:
            return near.at[behind - (zn - 5)]
        if whole or behind <= REACH:
            return far.at[behind - 3]
        return far.at[behind - 3 - (zn - 2 * REACH - 1)]

    def behind_of(way, hop):
        return hop if way == 0 else (zn - hop) % zn

    def to_core(behind, k):
        block = slab(behind).at[2 * c + k]
        return remote(block, block, cs.at[behind, k], cr.at[behind, k], (z, other, y))

    def from_core(behind, k):
        block = slab(behind).at[2 * (1 - c) + k]
        return remote(block, block, cs.at[behind, k], cr.at[behind, k], (z, other, y))

    def along(way, hop, k):
        return remote(
            slab(behind_of(way, hop - 1)).at[2 * c + k], slab(behind_of(way, hop)).at[2 * c + k],
            zs.at[way, hop, k], zr.at[way, hop, k], ((up, down)[way], op, y),
        )

    def hand_on(hop, turn):
        k = piece[turn]
        for way in range(2):
            if hop <= hops[way][turn]:
                if hop > 0:
                    along(way, hop, k).wait_recv()
                if hop < hops[way][turn]:
                    along(way, hop + 1, k).start()
                if hop > 0 or way == 0:
                    to_core(behind_of(way, hop), k).start()

    for turn in range(2):
        k = piece[turn]
        pltpu.make_async_copy(elements.at[0, k], near.at[0, 2 * c + k], own_recv.at[k]).wait()
        hand_on(0, turn)

    if whole:
        work = [z]
    else:
        found, early, late = assign(zn, z, pairs)
        flag[0] = found
        work = [jnp.maximum(early, 0), jnp.maximum(late, 0)]
    take_perambs.wait()

    def send_perambs(n):
        ps[n][y] = pv[work[n]]
        for d in range(1, 4):
            remote(ps[n].at[y], ps[n].at[y], qs.at[n, d], qr.at[n, d], (z, op, lax.rem(y + d, 4))).start()

    send_perambs(0)
    lane = iota((32, 128), 1) < 64
    low = iota((64, 128), 1) < 64
    bd[...] = jnp.zeros_like(bd)

    def matrices(n):
        for d in range(1, 4):
            remote(
                ps[n].at[y], ps[n].at[lax.rem(y + 4 - d, 4)], qs.at[n, d], qr.at[n, d], (z, op, y)
            ).wait_recv()

        def flat(l, carry, g):
            rows = ps[n][g, l].astype(F32)
            for t in range(32):
                s8[t * 8:t * 8 + 4, :] = rows[:, t * 128:(t + 1) * 128]
            for b in range(4):
                q = s8[pl.ds(b, 32, stride=8), :]
                r = pltpu.roll(q, 64, 1)
                n64[pl.ds(b * 64, 32, stride=2), :] = jnp.where(lane, q, r)
                n64[pl.ds(b * 64 + 1, 32, stride=2), :] = jnp.where(lane, r, q)
                qn[g, b, l] = n64[b * 64:(b + 1) * 64, :].astype(BF16)
            return carry

        for g in range(4):
            lax.fori_loop(0, 3, functools.partial(flat, g=g), 0)

        def blocks(b, carry):
            g, bb = b // 4, lax.rem(b, 4)
            q0s[pl.ds(b * 32, 32), :] = qn[g, bb, 0, pl.ds(32 * c, 32), :]
            q2 = qn[g, bb, 2]
            none = jnp.zeros_like(q2)
            for k in range(4):
                half = jnp.where(low, q2, none) if k % 2 == 0 else jnp.where(low, none, q2)
                bd[b, k * 64:(k + 1) * 64, (k // 2) * 128:(k // 2 + 1) * 128] = half
            return carry

        lax.fori_loop(0, 16, blocks, 0)
        row, column = iota((128, 128), 0), iota((128, 128), 1)
        for g in range(4):
            for lo in range(2):
                acc = jnp.zeros((64, 128), F32)
                for bb in range(4):
                    spot = (row < 64) & (lax.rem(row, 2) == lo) & (column == bb * 32 + row // 2)
                    acc += dot(qn[g, bb, 1], jnp.where(spot, 1.0, 0.0).astype(BF16))
                q1r[lo * 64:(lo + 1) * 64, g * 128:(g + 1) * 128] = acc.astype(BF16)

    def seek(time):
        behind = lax.rem(z + zn - time, zn)
        is_near = (behind <= 2) | (behind >= zn - 2)
        near_at = jnp.where(is_near, jnp.where(behind <= 2, behind, behind - (zn - 5)), 0)
        if whole:
            far_at = jnp.where(is_near, 0, behind - 3)
        else:
            far_at = jnp.where(behind <= REACH, behind - 3, behind - 3 - (zn - 2 * REACH - 1))
            far_at = jnp.clip(jnp.where(is_near, 0, far_at), 0, 2 * REACH - 5)
        return is_near, near_at, far_at

    def chip_at(d):
        xx, yy = lax.rem(x + d // 4, 4), lax.rem(y + d % 4, 4)
        return xx * 4 + yy, (z, 2 * xx + c, yy)

    def post(data, landed, send, recv):
        def one(d, carry):
            u, device = chip_at(d)
            remote(data.at[u], landed.at[chip], send.at[d], recv.at[chip], device).start()
            return carry

        return one

    def collect(landed, send, recv):
        def one(d, carry):
            e = lax.rem(chip + d, 16)
            remote(landed.at[e], landed.at[e], send.at[d], recv.at[e], (z, op, y)).wait_recv()
            return carry

        lax.fori_loop(1, 16, one, 0)

    def send_sink(n):
        is_near, near_at, far_at = seek(pairs[1, work[n]])
        for k in range(2):
            def lift(t, carry, k=k):
                columns = pl.ds(pl.multiple_of(t * 128, 128), 128)
                tile = jnp.where(is_near, near[near_at, 2 * c + k, :, columns].astype(F32),
                                 far[far_at, 2 * c + k, :, columns].astype(F32))
                t2[pl.ds(pl.multiple_of((k * 32 + t) * 24, 8), 16), :] = tile
                return carry

            lax.fori_loop(0, 32, lift, 0, unroll=8)

        def cut(u, carry):
            sink[n][u] = t2[pl.ds(u, 64, stride=24), :].astype(BF16)
            return carry

        lax.fori_loop(0, 16, cut, 0, unroll=8)
        send = post(sink[n], rsink[n], bsend.at[n], br.at[n])
        for d in FAR_CHIPS:
            send(d, 0)
        rsink[n][chip] = sink[n][chip]

    def step_one(n, only_near):
        is_near, near_at, far_at = seek(pairs[0, work[n]])

        def body(t, carry):
            columns = pl.ds(pl.multiple_of(t * 256, 256), 256)
            tile = near[near_at, :, :, columns]
            if not only_near:
                tile = jnp.where(is_near, tile.astype(F32), far[far_at, :, :, columns].astype(F32)).astype(BF16)
            first = dot(q0s[:, :64], tile.reshape(64, 256)).astype(BF16)
            v[:, t] = first.reshape(16, 32, 256)
            return carry

        lax.fori_loop(0, 16, body, 0, unroll=16)

    def step_two():
        def body(b, carry):
            second = dot(v[b].reshape(512, 256), bd[b], NT)
            for n in range(16):
                for h in range(2):
                    start = pl.multiple_of((b * 32 + n * 2 + h) * PITCH, 8)
                    t2[pl.ds(start, 32), :] = second[n * 32:(n + 1) * 32, h * 128:(h + 1) * 128]
            return carry

        lax.fori_loop(0, 16, body, 0, unroll=16)

    def step_three(n):
        def body(d, carry):
            u = chip_at(d)[0]
            left = t2[pl.ds(u, 512, stride=PITCH), :].astype(BF16)
            right = t2[pl.ds(u + 16, 512, stride=PITCH), :].astype(BF16)
            both = dot(q1r[...], jnp.concatenate([left, right], axis=1))
            even = both[:64, :128] + pltpu.roll(both[64:, :128], 64, 1)
            odd = pltpu.roll(both[:64, 128:], 64, 1) + both[64:, 128:]
            prod[n][u] = jnp.where(low, even, odd).astype(BF16)
            return carry

        order = FAR_CHIPS + [0]
        send = post(prod[n], rprod[n], asend.at[n], ar.at[n])
        for start in (0, 4, 8, 12):
            for d in order[start:start + 4]:
                body(d, 0)
            for d in order[start:start + 4]:
                if d:
                    send(d, 0)
        rprod[n][chip] = prod[n][chip]

    if whole:
        for hop in range(1, max(hops[0]) + 1):
            for turn in range(2):
                hand_on(hop, turn)
            if hop == 1:
                matrices(0)
        for behind in held:
            for k in range(2):
                from_core(behind, k).wait_recv()
    else:
        for turn in range(2):
            hand_on(1, turn)
        matrices(0)
        for turn in range(2):
            hand_on(2, turn)
        send_perambs(1)
        close = [b for b in held if b <= 2 or b >= zn - 2]
        for behind in close:
            for k in range(2):
                from_core(behind, k).wait_recv()
        step_one(0, True)
        hand_on(3, 0)
        step_two()
        hand_on(3, 1)
        step_three(0)
        hand_on(4, 0)
        matrices(1)
        hand_on(4, 1)
        for away in (REACH, zn - REACH):
            pl.semaphore_signal(
                token, inc=1, device_id=(lax.rem(z + away, zn), op, y), device_id_type=MESH
            )
        for behind in held:
            if behind not in close:
                for k in range(2):
                    from_core(behind, k).wait_recv()

    last = slots - 1
    for n in reversed(range(slots)):
        send_sink(n)
    step_one(last, False)
    step_two()
    step_three(last)

    lane16 = iota((16, 128), 1) < 64
    wl, wj = iota((16, 128), 0), iota((16, 128), 1)

    def contract(n):
        collect(rsink[n], bsend.at[n], br.at[n])
        for i in range(16):
            t2[i * 72:i * 72 + 64, :] = rsink[n][i].astype(F32)
        for r in range(64):
            ks[:, r * 128:(r + 1) * 128] = t2[pl.ds(r, 16, stride=72), :].astype(BF16)
        collect(rprod[n], asend.at[n], ar.at[n])
        for j in range(16):
            t2[j * 72:j * 72 + 64, :] = rprod[n][j].astype(F32)
        for t in range(32):
            a = t2[pl.ds(2 * t, 16, stride=72), :]
            b = t2[pl.ds(2 * t + 1, 16, stride=72), :]
            kp[:, t * 128:(t + 1) * 128] = jnp.where(lane16, a, pltpu.roll(b, 64, 1)).astype(BF16)
            kp[:, (32 + t) * 128:(33 + t) * 128] = jnp.where(lane16, pltpu.roll(a, 64, 1), b).astype(BF16)
        square = dot(ks[...], kp[...], NT)
        table = dot(square, jnp.where(wl == lax.rem(wj, 16), 1.0, 0.0).astype(F32), precision=lax.Precision.HIGHEST)
        mine = jnp.where(wj // 16 == lax.rem(wl, 8), table, 0.0)
        return jnp.sum(mine.reshape(2, 8, 128), axis=1)

    tables = [contract(n) for n in range(slots)]
    place = op * 4 + y
    if whole:
        part[place] = tables[0]
    else:
        pl.semaphore_wait(token, 2)
        for d in sorted(range(zn), key=lambda d: -min(d, zn - d)):
            p = lax.rem(z + d, zn)
            zout[d] = jnp.where(early == p, tables[0], 0.0) + jnp.where(late == p, tables[1], 0.0)
            if d > 0:
                remote(zout.at[d], zin.at[d], ws.at[d], wr.at[d], (p, op, y)).start()
        zin[0] = zout[0]
        for d in range(1, zn):
            remote(zout.at[d], zin.at[d], ws.at[d], wr.at[d], (z, op, y)).wait_recv()
        part[place] = jnp.sum(zin[...], axis=0)

    def tell(d):
        o, s = lax.rem(op + d // 4, 8), lax.rem(y + d % 4, 4)
        return remote(part.at[place], part.at[place], rs.at[d], rr.at[d], (z, o, s))

    def told(d):
        o, s = lax.rem(op + 8 - d // 4, 8), lax.rem(y + 4 - d % 4, 4)
        return remote(part.at[place], part.at[o * 4 + s], rs.at[d], rr.at[d], (z, op, y))

    for d in FAR_PLACES:
        tell(d).start()
    for d in range(1, 32):
        told(d).wait_recv()
    out[...] = jnp.sum(part[...], axis=0)

    for k in range(2):
        @pl.when(2 * c + k != y)
        def _(k=k):
            remote(elements.at[0, k], near.at[0, y], own_send.at[k], own_recv.at[k], (z, op, y)).wait_send()

        for way in range(2):
            for hop in range(1, hops[way][k] + 1):
                along(way, hop, piece[k]).wait_send()
        for behind in held:
            to_core(behind, k).wait_send()
    for n in range(slots):
        for d in range(1, 4):
            remote(ps[n].at[y], ps[n].at[y], qs.at[n, d], qr.at[n, d], (z, op, y)).wait_send()

        def left(d, carry, n=n):
            remote(sink[n].at[0], rsink[n].at[0], bsend.at[n, d], br.at[n, 0], (z, op, y)).wait_send()
            remote(prod[n].at[0], rprod[n].at[0], asend.at[n, d], ar.at[n, 0], (z, op, y)).wait_send()
            return carry

        lax.fori_loop(1, 16, left, 0)

    for d in range(1, 32):
        tell(d).wait_send()
    if not whole:
        for d in range(1, zn):
            remote(zout.at[d], zin.at[d], ws.at[d], wr.at[d], (z, op, y)).wait_send()


def call(zn, whole, pairs, elements, perambs):
    dma = pltpu.SemaphoreType.DMA
    slots = 1 if whole else 2
    far = zn - 5 if whole else 2 * REACH - 4
    out_shape = [jax.ShapeDtypeStruct((2, 128), F32)]
    out_specs = [pl.BlockSpec(memory_space=pltpu.VMEM)]
    if not whole:
        out_shape.append(jax.ShapeDtypeStruct((1,), jnp.int32))
        out_specs.append(pl.BlockSpec(memory_space=pltpu.SMEM))
    return pl.pallas_call(
        functools.partial(kernel, zn, whole),
        out_shape=out_shape,
        in_specs=[
            pl.BlockSpec(memory_space=pltpu.SMEM),
            pl.BlockSpec(memory_space=pl.ANY),
            pl.BlockSpec(memory_space=pl.ANY),
        ],
        out_specs=out_specs,
        scratch_shapes=[
            *[pltpu.VMEM((4, 3, 4, 4096), BF16)] * slots,
            *[pltpu.VMEM((16, 64, 128), BF16)] * (4 * slots),
            pltpu.VMEM((5, 4, 16, 4096), BF16),
            pltpu.VMEM((far, 4, 16, 4096), BF16),
            pltpu.VMEM((16, 3, 4, 4096), BF16),
            pltpu.VMEM((272, 128), F32),
            pltpu.VMEM((272, 128), F32),
            pltpu.VMEM((4, 4, 3, 64, 128), BF16),
            pltpu.VMEM((512, 128), BF16),
            pltpu.VMEM((16, 256, 256), BF16),
            pltpu.VMEM((128, 512), BF16),
            pltpu.VMEM((16, 16, 32, 256), BF16),
            pltpu.VMEM((512 * PITCH + 64, 128), F32),
            pltpu.VMEM((16, 8192), BF16),
            pltpu.VMEM((16, 8192), BF16),
            pltpu.VMEM((32, 2, 128), F32),
            pltpu.VMEM((zn, 2, 128), F32),
            pltpu.VMEM((zn, 2, 128), F32),
            dma, dma((2,)), dma((2,)),
            dma((2, zn, 2)), dma((2, zn, 2)), dma((zn, 2)), dma((zn, 2)),
            dma((slots, 4)), dma((slots, 4)),
            dma((slots, 16)), dma((slots, 16)), dma((slots, 16)), dma((slots, 16)), dma((32,)), dma((32,)),
            dma((zn,)), dma((zn,)), pltpu.SemaphoreType.REGULAR,
        ],
        compiler_params=pltpu.CompilerParams(
            collective_id=1 if whole else 0, has_side_effects=True, vmem_limit_bytes=56 * 1024 * 1024
        ),
    )(pairs, elements, perambs)


def solution(mesh):
    zn = mesh.shape["tm"]

    def body(pairs, elements, perambs):
        given = (pairs.T, elements, perambs.transpose(0, 2, 1, 3))
        table, found = call(zn, False, *given)
        table = lax.cond(found[0] == 1, lambda: table, lambda: call(zn, True, *given)[0])
        return table.reshape(1, 16, 16)

    placed = (P(), P("tm", "op", "spin", None), P(None, "spin", None, None))
    return jax.shard_map(
        body, mesh=mesh, in_specs=placed, out_specs=P("tm", None, None), check_vma=False
    )
```
